32 devices in a mesh: chan: 4 (over x, core), ctx: 8 (over z, y).
Axes of the slice: x: 2, y: 2, z: 4, core: 2. Of those that a mesh axis runs over, the one named last changes fastest.
Arguments:
- queries: bfloat16 [1024, 8192], P('ctx', 'chan'), may hold values from -6 to 6
- keys: bfloat16 [1024, 8192], P('ctx', 'chan'), may hold values from -6 to 6
- values: bfloat16 [1024, 8192], P('ctx', 'chan'), may hold values from -6 to 6
- filters: bfloat16 [4, 1024], P(None, 'ctx'), may hold values from -0.1875 to 0.1875
- cotangent: bfloat16 [1024, 8192], P('ctx', 'chan'), may hold values from -6 to 6
Outputs:
- output: bfloat16 [1024, 8192], P('ctx', 'chan')
- query_grad: bfloat16 [1024, 8192], P('ctx', 'chan')
- key_grad: bfloat16 [1024, 8192], P('ctx', 'chan')
- value_grad: bfloat16 [1024, 8192], P('ctx', 'chan')
- filter_grad: float32 [4, 1024], P(None, 'ctx')
The draws below stay inside these ranges and needn't reach their ends.
All inputs are finite; a program needn't handle non-finite values.
Results may differ from the reference program's by a relative error of at most 0.015.
Values may be sent and summed in bfloat16 or wider, within the bound.
No kernel may reach another device: no remote copies, remote signals or barrier semaphores. Data moves between devices by JAX's collectives and lax.ppermute only.
A program may use at most 64 MiB of HBM per device.

```python
import jax
import jax.numpy as jnp
from jax import lax

D = 8192
NFILT = 4
TOKENS = 1024


def levels(key, dims, pieces, least, top_value):
    factor_of, own = 1.0, jax.random.fold_in(key, 6)
    for dim, parts in pieces:
        draws = jnp.exp(jax.random.uniform(jax.random.fold_in(own, dim), (parts,), jnp.float32, least / len(pieces), top_value / len(pieces)))
        factor_of = factor_of * jnp.repeat(draws, dims[dim] // parts).reshape([-1 if axis == dim else 1 for axis in range(len(dims))])
    return factor_of


def centred(stream_key, extent, spread, reach, cuts=(), kind=jnp.bfloat16):
    result = spread * jax.random.normal(stream_key, extent, jnp.float32)
    if cuts:
        result = result * levels(stream_key, extent, cuts, -0.22, 0.18)
    return jnp.clip(result, -reach, reach).astype(kind)


def setup_inputs(seed: int = 0) -> dict:
    streams_of = jax.random.split(jax.random.key(seed), 6)
    queries = centred(streams_of[0], (TOKENS, D), 1.0, 6.0, ((0, 8), (1, 4)))
    keys = centred(streams_of[1], (TOKENS, D), 1.0, 6.0, ((0, 8), (1, 4)))
    values = centred(streams_of[2], (TOKENS, D), 1.0, 6.0, ((0, 8), (1, 4)))
    filters = centred(streams_of[3], (NFILT, TOKENS), TOKENS ** -0.5, 0.1875, ((1, 8),))
    cotangent = centred(streams_of[4], (TOKENS, D), 1.0, 6.0, ((0, 8), (1, 4)))
    return {"queries": queries, "keys": keys, "values": values, "filters": filters, "cotangent": cotangent}


def reference(queries, keys, values, filters, cotangent):
    tokens, width = queries.shape
    nfil = filters.shape[0]
    gated = (keys.astype(jnp.float32) * values.astype(jnp.float32)).astype(jnp.bfloat16)
    back = (cotangent.astype(jnp.float32) * queries.astype(jnp.float32)).astype(jnp.bfloat16)
    gated_cols = gated.reshape(tokens, width // nfil, nfil)
    back_cols = back.reshape(tokens, width // nfil, nfil)
    steps = jnp.arange(tokens, dtype=jnp.int32)
    lagged = steps[:, None] - steps[None, :]

    def per_filter(index):
        taps_row = lax.dynamic_index_in_dim(filters, index, 0, keepdims=False)
        picked = taps_row[jnp.clip(lagged, 0, tokens - 1)]
        toeplitz = jnp.where(lagged >= 0, picked, jnp.zeros_like(picked))
        gated_f = lax.dynamic_index_in_dim(gated_cols, index, 2, keepdims=False)
        back_f = lax.dynamic_index_in_dim(back_cols, index, 2, keepdims=False)
        mixed_f = jnp.dot(toeplitz, gated_f, preferred_element_type=jnp.float32)
        grad_f = jnp.dot(toeplitz.T, back_f, preferred_element_type=jnp.float32)
        product = jnp.dot(back_f, gated_f.T, preferred_element_type=jnp.float32)
        flipped = product[:, ::-1]
        padded = jnp.pad(flipped, ((0, 0), (0, tokens)))
        flat = padded.reshape(tokens * 2 * tokens)[: tokens * (2 * tokens - 1)]
        sums = jnp.sum(flat.reshape(tokens, 2 * tokens - 1), axis=0)
        return mixed_f, grad_f, sums[tokens - 1:]

    mixed_all, grad_all, lag_all = lax.map(per_filter, jnp.arange(nfil, dtype=jnp.int32))
    mixed = jnp.transpose(mixed_all, (1, 2, 0)).reshape(tokens, width)
    gated_grad = jnp.transpose(grad_all, (1, 2, 0)).reshape(tokens, width)
    scale = (tokens * (width // nfil)) ** -0.5
    filter_grad = lag_all * scale
    output = (queries.astype(jnp.float32) * mixed).astype(jnp.bfloat16)
    query_grad = (cotangent.astype(jnp.float32) * mixed).astype(jnp.bfloat16)
    key_grad = (gated_grad * values.astype(jnp.float32)).astype(jnp.bfloat16)
    value_grad = (gated_grad * keys.astype(jnp.float32)).astype(jnp.bfloat16)
    return (output, query_grad, key_grad, value_grad, filter_grad)
```

```python
import functools

import jax
import jax.numpy as jnp
from jax import lax
from jax.experimental import pallas as pl
from jax.experimental.pallas import tpu as pltpu
from jax.sharding import PartitionSpec as P

D = 8192
NFILT = 4
LANES = 128


def exchange(size, reverse, dtype):
    row = lax.broadcasted_iota(jnp.int32, (size, size), 0)
    col = lax.broadcasted_iota(jnp.int32, (size, size), 1)
    target = jnp.where(reverse, size - 1 - row, row)
    return jnp.where(col == target, 1.0, 0.0).astype(jnp.float32).astype(dtype)


def exact_rows(matrix, values):
    return jnp.dot(matrix, values, preferred_element_type=jnp.float32).astype(jnp.bfloat16)


def gate_kernel(half, slim, me_ref, q_ref, k_ref, v_ref, g_ref, *refs):
    outs, (within, across) = refs[:-2], refs[-2:]
    rows = q_ref.shape[0]
    me = me_ref[0]
    upper = me >= half
    gated = (k_ref[...].astype(jnp.float32) * v_ref[...].astype(jnp.float32)).astype(jnp.bfloat16)
    back = (g_ref[...].astype(jnp.float32) * q_ref[...].astype(jnp.float32)).astype(jnp.bfloat16)
    first = jnp.where(upper, gated, back)
    second = jnp.where(upper, back, gated)
    turn = exchange(rows, upper, jnp.bfloat16)
    turn_other = exchange(rows, jnp.logical_not(upper), jnp.bfloat16)
    within[0:rows, :] = exact_rows(turn, first)
    within[rows : 2 * rows, :] = exact_rows(turn, second)
    across[...] = exact_rows(turn_other, second)
    for step in range(2 * half):
        part = (me ^ step) & (half - 1)
        lanes = pl.ds(pl.multiple_of(part * slim, LANES), slim)
        source = within if step < half else across
        outs[step][...] = source[:, lanes]


def taps_kernel(me_ref, taps_ref, near_ref, far_ref, line):
    blocks = line.shape[1] // LANES
    nfil, size, total = near_ref.shape
    for step in range(blocks):
        place = pl.multiple_of((me_ref[0] ^ step) * LANES, LANES)
        line[:, pl.ds(place, LANES)] = taps_ref[8 * step : 8 * step + 8, :]
    row = lax.broadcasted_iota(jnp.int32, (size, total), 0)
    col = lax.broadcasted_iota(jnp.int32, (size, total), 1)
    for index in range(nfil):
        spread = jnp.broadcast_to(line[index : index + 1, :], (size, total))
        rolled = pltpu.roll(spread, 0, 1, stride=1, stride_axis=0)
        band = jnp.where(col >= row, rolled, 0.0)
        near_ref[index] = band.astype(jnp.bfloat16)
        reach = far_ref.shape[2] // size
        for block in range(reach):
            piece = band[:, (reach - 1 - block) * size : (reach - block) * size]
            far_ref[index, :, block * size : (block + 1) * size] = piece.T.astype(jnp.bfloat16)


def assemble(half, me, upper, arrived, first_ref, second_ref):
    rows = arrived[0].shape[0] // 2
    flip = jnp.where(upper, half - 1, 0)
    slots = []
    for step in range(2 * half):
        slot = ((me ^ step) & (half - 1)) ^ flip
        slots.append(slot)
        if step < half:
            where = pl.ds(pl.multiple_of(slot * rows, rows), rows)
            first_ref[where, :] = arrived[step][0:rows, :]
            second_ref[where, :] = arrived[step][rows : 2 * rows, :]
        else:
            where = pl.ds(pl.multiple_of((slot + half) * rows, rows), rows)
            first_ref[where, :] = arrived[step][...]
    return slots


def lane_mask(width, nfil, index):
    lane = lax.broadcasted_iota(jnp.int32, (1, width), 1)
    return jnp.where(lane % nfil == index, 1.0, 0.0).astype(jnp.bfloat16)


def conv_kernel(half, me_ref, *refs):
    arrived = refs[: 2 * half]
    near_ref, far_ref = refs[2 * half : 2 * half + 2]
    outs = refs[2 * half + 2 : 3 * half + 2]
    first_ref, second_ref, result_ref = refs[3 * half + 2 :]
    nfil, size, total = near_ref.shape
    width = first_ref.shape[1]
    own = second_ref.shape[0]
    rows = own // half
    me = me_ref[0]
    upper = me >= half
    slots = assemble(half, me, upper, arrived, first_ref, second_ref)
    masks = [lane_mask(width, nfil, index) for index in range(nfil)]
    for top in range(0, own, size):
        acc = jnp.zeros((size, width), jnp.float32)
        for index in range(nfil):
            acc += jnp.dot(
                near_ref[index, :, 0 : total - top],
                first_ref[top:total, :] * masks[index],
                preferred_element_type=jnp.float32,
            )
        result_ref[0, top : top + size, :] = acc.astype(jnp.bfloat16)
        acc = jnp.zeros((size, width), jnp.float32)
        for index in range(nfil):
            acc += jnp.dot(
                far_ref[index, :, own - size - top : own],
                second_ref[0 : top + size, :] * masks[index],
                preferred_element_type=jnp.float32,
            )
        result_ref[1, top : top + size, :] = acc.astype(jnp.bfloat16)
    for step in range(half):
        where = pl.ds(pl.multiple_of(slots[step] * rows, rows), rows)
        outs[step][0:rows, :] = result_ref[0, where, :]
        outs[step][rows : 2 * rows, :] = result_ref[1, where, :]


def lag_kernel(half, me_ref, *refs):
    arrived = refs[: 2 * half]
    out_ref = refs[2 * half]
    first_ref, second_ref = refs[2 * half + 1 :]
    total, width = first_ref.shape
    own = second_ref.shape[0]
    rows = own // half
    nfil = NFILT
    me = me_ref[0]
    upper = me >= half
    assemble(half, me, upper, arrived, first_ref, second_ref)
    turn = exchange(rows, True, jnp.bfloat16)
    share = width // 2
    lanes = pl.ds(pl.multiple_of(jnp.where(upper, share, 0), LANES), share)
    contract = (((1,), (1,)), ((), ()))
    flipped = [exact_rows(turn, second_ref[b * rows : (b + 1) * rows, :]) for b in range(half)]
    halves = [exact_rows(turn, second_ref[b * rows : (b + 1) * rows, lanes]) for b in range(half)]
    for index in range(nfil):
        mask = lane_mask(width, nfil, index)
        half_mask = lane_mask(share, nfil, index)
        inner = first_ref[0:own, :] * mask
        outer = first_ref[own:total, lanes] * half_mask
        acc = jnp.zeros((rows, total + rows), jnp.float32)
        for block in range(half):
            start = block * rows
            near = lax.dot_general(
                flipped[block], inner[start:own], contract, preferred_element_type=jnp.float32
            )
            far = lax.dot_general(
                halves[block], outer, contract, preferred_element_type=jnp.float32
            )
            pieces = [near, far, jnp.zeros((rows, start + rows), jnp.float32)]
            acc = acc + jnp.concatenate(pieces, axis=1)
        rolled = pltpu.roll(acc, 0, 1, stride=1, stride_axis=0)
        sums = jnp.sum(rolled, axis=0, keepdims=True)
        sums = jnp.broadcast_to(sums, (8, total + rows))
        lags = pltpu.roll(sums, total + 1, 1)
        out_ref[index : index + 1, :] = lags[0:1, 0:total]
    out_ref[nfil:8, :] = jnp.zeros((8 - nfil, total), jnp.float32)


def final_kernel(half, slim, me_ref, q_ref, k_ref, v_ref, g_ref, *refs):
    results = refs[:half]
    out_ref, dq_ref, dk_ref, dv_ref = refs[half : half + 4]
    (joined,) = refs[half + 4 :]
    rows = q_ref.shape[0]
    me = me_ref[0]
    upper = me >= half
    turn = exchange(rows, upper, jnp.bfloat16)
    for step in range(half):
        part = (me ^ step) & (half - 1)
        lanes = pl.ds(pl.multiple_of(part * slim, LANES), slim)
        joined[:, lanes] = results[step][...]
    first = jnp.dot(turn, joined[0:rows, :], preferred_element_type=jnp.float32)
    second = jnp.dot(turn, joined[rows : 2 * rows, :], preferred_element_type=jnp.float32)
    mixed = jnp.where(upper, first, second)
    grad = jnp.where(upper, second, first)
    out_ref[...] = (q_ref[...].astype(jnp.float32) * mixed).astype(jnp.bfloat16)
    dq_ref[...] = (g_ref[...].astype(jnp.float32) * mixed).astype(jnp.bfloat16)
    dk_ref[...] = (v_ref[...].astype(jnp.float32) * grad).astype(jnp.bfloat16)
    dv_ref[...] = (k_ref[...].astype(jnp.float32) * grad).astype(jnp.bfloat16)


def swap(value, step, count):
    return lax.ppermute(value, "ctx", [(i, i ^ step) for i in range(count)])


def call(kernel, outs, scratch, flops, nbytes, *args):
    return pl.pallas_call(
        kernel,
        out_shape=outs,
        in_specs=[pl.BlockSpec(memory_space=pltpu.SMEM)]
        + [pl.BlockSpec(memory_space=pltpu.VMEM)] * (len(args) - 1),
        out_specs=jax.tree.map(lambda _: pl.BlockSpec(memory_space=pltpu.VMEM), outs),
        scratch_shapes=scratch,
        compiler_params=pltpu.CompilerParams(vmem_limit_bytes=48 * 2**20),
        cost_estimate=pl.CostEstimate(flops=flops, bytes_accessed=nbytes, transcendentals=0),
    )(*args)


def halves_plan(count, chans, queries, keys, values, filters, cotangent):
    rows, width = queries.shape
    nfil = filters.shape[0]
    half = count // 2
    slim = width // half
    total = count * rows
    own = half * rows
    size = min(256, own)
    low = jnp.bfloat16
    shape = jax.ShapeDtypeStruct
    me = lax.axis_index("ctx")
    where = me.astype(jnp.int32).reshape(1)

    taps = jnp.pad(filters.astype(jnp.float32), ((0, 8 - nfil), (0, 0)))
    step = 1
    while step < count:
        taps = jnp.concatenate([taps, swap(taps, step, count)], axis=0)
        step *= 2

    sent = call(
        functools.partial(gate_kernel, half, slim),
        [shape((2 * rows if k < half else rows, slim), low) for k in range(count)],
        [pltpu.VMEM((2 * rows, width), low), pltpu.VMEM((rows, width), low)],
        6 * rows * rows * width,
        14 * rows * width,
        where, queries, keys, values, cotangent,
    )
    arrived = [sent[0]] + [swap(sent[k], k, count) for k in range(1, count)]

    near, far = call(
        taps_kernel,
        [shape((nfil, size, total), low), shape((nfil, size, own), low)],
        [pltpu.VMEM((8, total), jnp.float32)],
        nfil * size * total * 8,
        nfil * size * total * 4,
        where, taps,
    )
    results = call(
        functools.partial(conv_kernel, half),
        [shape((2 * rows, slim), low)] * half,
        [
            pltpu.VMEM((total, slim), low),
            pltpu.VMEM((own, slim), low),
            pltpu.VMEM((2, own, slim), low),
        ],
        2 * nfil * own * slim * (total + own),
        4 * total * slim,
        where, *arrived, near, far,
    )
    returned = [results[0]] + [swap(results[k], k, count) for k in range(1, half)]
    lags = call(
        functools.partial(lag_kernel, half),
        shape((8, total), jnp.float32),
        [pltpu.VMEM((total, slim), low), pltpu.VMEM((own, slim), low)],
        2 * nfil * own * slim * total,
        4 * total * slim,
        where, *arrived,
    )
    step = 1
    while step < chans:
        lags = lags + lax.ppermute(lags, "chan", [(i, i ^ step) for i in range(chans)])
        step *= 2
    step = half
    while step:
        extent = lags.shape[1] // 2
        low_part, high_part = lags[:, :extent], lags[:, extent:]
        mine_high = (me & step) != 0
        keep = jnp.where(mine_high, high_part, low_part)
        send = jnp.where(mine_high, low_part, high_part)
        lags = keep + swap(send, step, count)
        step //= 2
    scale = (total * (D // NFILT)) ** (-0.5)
    filter_grad = lags[:nfil] * scale

    outs = call(
        functools.partial(final_kernel, half, slim),
        [shape((rows, width), low)] * 4,
        [pltpu.VMEM((2 * rows, width), low)],
        4 * rows * rows * width,
        20 * rows * width,
        where, queries, keys, values, cotangent, *returned,
    )
    return (*outs, filter_grad)


def toeplitz(padded, base, height, breadth):
    middle = padded.shape[1] // 2
    span = height + breadth - 1
    window = lax.dynamic_slice_in_dim(padded, middle + base - breadth + 1, span, 1)
    flipped = window[:, ::-1]
    tiled = jnp.tile(flipped, (1, height + 1))
    flat = tiled[:, height - 1 : height - 1 + height * (span - 1)]
    return flat.reshape(padded.shape[0], height, span - 1)[:, :, :breadth]


def diagonal_sums(product):
    nfil, height, breadth = product.shape
    stride = height + breadth
    flipped = product[:, :, ::-1]
    padded = jnp.pad(flipped, ((0, 0), (0, 0), (0, height)))
    flat = padded.reshape(nfil, height * stride)[:, : height * (stride - 1)]
    return jnp.sum(flat.reshape(nfil, height, stride - 1), axis=1)


def add_lags(lag_acc, sums, first_lag):
    middle = lag_acc.shape[1] // 2
    where = middle + first_lag
    current = lax.dynamic_slice_in_dim(lag_acc, where, sums.shape[1], 1)
    return lax.dynamic_update_slice_in_dim(lag_acc, current + sums, where, 1)


def channel_plan(queries, keys, values, filters, cotangent):
    rows, width = queries.shape
    nfil = filters.shape[0]
    gated = (keys.astype(jnp.float32) * values.astype(jnp.float32)).astype(jnp.bfloat16)
    back = (cotangent.astype(jnp.float32) * queries.astype(jnp.float32)).astype(jnp.bfloat16)
    taps = lax.all_gather(filters, "ctx", axis=1, tiled=True)
    total = taps.shape[1]
    padded = jnp.concatenate([jnp.zeros_like(taps), taps], axis=1)
    lag_start = jnp.zeros((nfil, 2 * total), jnp.float32)
    chan_gated, chan_back = (
        lax.all_to_all(gated, "ctx", split_axis=1, concat_axis=0, tiled=True),
        lax.all_to_all(back, "ctx", split_axis=1, concat_axis=0, tiled=True),
    )
    blocks = total // rows
    slim = chan_gated.shape[1] // nfil
    gated_cols = chan_gated.reshape(blocks, rows, slim, nfil)
    back_cols = chan_back.reshape(blocks, rows, slim, nfil)
    gated_pad = jnp.concatenate([jnp.zeros_like(gated_cols), gated_cols], axis=0)
    back_pad = jnp.concatenate([back_cols, jnp.zeros_like(back_cols)], axis=0)

    def turn(offset, carry):
        mixed_acc, grad_acc, lag_acc = carry
        tile = toeplitz(padded, offset * rows, rows, rows)
        earlier = lax.dynamic_slice_in_dim(gated_pad, blocks - offset, blocks, 0)
        later = lax.dynamic_slice_in_dim(back_pad, offset, blocks, 0)
        mixed_acc = mixed_acc + jnp.einsum(
            "fst,ntcf->nscf", tile, earlier, preferred_element_type=jnp.float32
        )
        grad_acc = grad_acc + jnp.einsum(
            "fst,nscf->ntcf", tile, later, preferred_element_type=jnp.float32
        )
        product = jnp.einsum(
            "nscf,ntcf->fst", back_cols, earlier, preferred_element_type=jnp.float32
        )
        lag_acc = add_lags(lag_acc, diagonal_sums(product), offset * rows - rows + 1)
        return (mixed_acc, grad_acc, lag_acc)

    blank = jnp.zeros((blocks, rows, slim, nfil), jnp.float32)
    mixed_acc, grad_acc, lag_part = lax.fori_loop(0, blocks, turn, (blank, blank, lag_start))
    mixed_chan = mixed_acc.reshape(total, slim * nfil)
    grad_chan = grad_acc.reshape(total, slim * nfil)
    mixed, gated_grad = (
        lax.all_to_all(mixed_chan, "ctx", split_axis=0, concat_axis=1, tiled=True),
        lax.all_to_all(grad_chan, "ctx", split_axis=0, concat_axis=1, tiled=True),
    )
    lag_share = lax.psum_scatter(
        lag_part[:, total:].astype(jnp.bfloat16), "ctx", scatter_dimension=1, tiled=True
    ).astype(jnp.float32)
    lag_total = lax.psum(lag_share, "chan")
    scale = (total * (D // NFILT)) ** (-0.5)
    filter_grad = lag_total * scale
    output = (queries.astype(jnp.float32) * mixed).astype(jnp.bfloat16)
    query_grad = (cotangent.astype(jnp.float32) * mixed).astype(jnp.bfloat16)
    key_grad = (gated_grad * values.astype(jnp.float32)).astype(jnp.bfloat16)
    value_grad = (gated_grad * keys.astype(jnp.float32)).astype(jnp.bfloat16)
    return (output, query_grad, key_grad, value_grad, filter_grad)


def solution(mesh):
    count, chans = mesh.shape["ctx"], mesh.shape["chan"]

    def shards(queries, keys, values, filters, cotangent):
        width = queries.shape[1]
        quarter = width // max(count // 2, 1)
        if count > 2 and quarter % (2 * LANES) == 0 and queries.shape[0] == LANES:
            return halves_plan(count, chans, queries, keys, values, filters, cotangent)
        return channel_plan(queries, keys, values, filters, cotangent)

    wide = P("ctx", "chan")
    return jax.shard_map(
        shards,
        mesh=mesh,
        in_specs=(wide, wide, wide, P(None, "ctx"), wide),
        out_specs=(wide, wide, wide, wide, P(None, "ctx")),
        check_vma=False,
    )
```

```python
import functools

import jax
import jax.numpy as jnp
from jax import lax
from jax.experimental import pallas as pl
from jax.experimental.pallas import tpu as pltpu
from jax.sharding import PartitionSpec as P

D = 8192
NFILT = 4
LANES = 128
GRANT = 24 * 2**20


def exchange(size, reverse, dtype):
    row = lax.broadcasted_iota(jnp.int32, (size, size), 0)
    col = lax.broadcasted_iota(jnp.int32, (size, size), 1)
    target = jnp.where(reverse, size - 1 - row, row)
    return jnp.where(col == target, 1.0, 0.0).astype(jnp.float32).astype(dtype)


def exact_rows(matrix, values):
    return jnp.dot(matrix, values, preferred_element_type=jnp.float32).astype(jnp.bfloat16)


def gate_kernel(half, slim, me_ref, q_ref, k_ref, v_ref, g_ref, *refs):
    outs, (pair_ref, held, sems) = refs[:-3], refs[-3:]
    rows = q_ref.shape[0]
    me = me_ref[0]
    upper = me >= half
    copies = []
    for step in range(half):
        part = (me ^ step) & (half - 1)
        lanes = pl.ds(pl.multiple_of(part * slim, LANES), slim)
        copies.append([])
        for index, ref in enumerate((q_ref, k_ref, v_ref, g_ref)):
            copy = pltpu.make_async_copy(
                ref.at[:, lanes], held.at[step, index], sems.at[step, index]
            )
            copy.start()
            copies[step].append(copy)
    turn_other = exchange(rows, jnp.logical_not(upper), jnp.bfloat16)
    for step in range(half):
        for copy in copies[step]:
            copy.wait()
        q, k, v, g = [held[step, index].astype(jnp.float32) for index in range(4)]
        gated = (k * v).astype(jnp.bfloat16)
        back = (g * q).astype(jnp.bfloat16)
        second = jnp.where(upper, back, gated)
        pair_ref[step, 0] = jnp.where(upper, gated, back)
        pair_ref[step, 1] = second
        outs[step][...] = exact_rows(turn_other, second)


def bundle_kernel(half, me_ref, mine_ref, other_ref, pair_ref, *outs):
    rows = pair_ref.shape[2]
    turn = exchange(rows, me_ref[0] >= half, jnp.bfloat16)
    both = jnp.concatenate([mine_ref[...], other_ref[...]], axis=0).astype(jnp.bfloat16)
    for step in range(half):
        outs[step][0:rows, :] = exact_rows(turn, pair_ref[step, 0])
        outs[step][rows : 2 * rows, :] = exact_rows(turn, pair_ref[step, 1])
        outs[step][2 * rows :, :] = jnp.zeros((16, outs[step].shape[1]), jnp.bfloat16)
        outs[step][2 * rows :, 0:LANES] = both


def fill_bands(half, me, arrived, near_ref, far_ref, line):
    nfil, size, total = near_ref.shape
    for step in range(half):
        both = arrived[step][arrived[step].shape[0] - 16 :, 0:LANES].astype(jnp.float32)
        for index, source in enumerate((me ^ step, me ^ step ^ half)):
            place = pl.multiple_of(source * LANES, LANES)
            line[:, pl.ds(place, LANES)] = both[8 * index : 8 * index + 8, :]
    row = lax.broadcasted_iota(jnp.int32, (size, total), 0)
    col = lax.broadcasted_iota(jnp.int32, (size, total), 1)
    reach = far_ref.shape[2] // size
    for index in range(nfil):
        spread = jnp.broadcast_to(line[index : index + 1, :], (size, total))
        rolled = pltpu.roll(spread, 0, 1, stride=1, stride_axis=0)
        band = jnp.where(col >= row, rolled, 0.0)
        near_ref[index] = band.astype(jnp.bfloat16)
        for block in range(reach):
            piece = band[:, (reach - 1 - block) * size : (reach - block) * size]
            far_ref[index, :, block * size : (block + 1) * size] = piece.T.astype(jnp.bfloat16)


def slot_of(half, me, step):
    return ((me ^ step) & (half - 1)) ^ jnp.where(me >= half, half - 1, 0)


def rows_at(slot, rows):
    return pl.ds(pl.multiple_of(slot * rows, rows), rows)


def add_lags_of(first, flipped, mask, start, width, acc):
    near = lax.dot_general(
        flipped, first * mask, (((1,), (1,)), ((), ())), preferred_element_type=jnp.float32
    )
    rows, reach = near.shape
    pieces = [near, jnp.zeros((rows, width - start - reach), jnp.float32)]
    if start:
        pieces = [jnp.zeros((rows, start), jnp.float32)] + pieces
    return acc + jnp.concatenate(pieces, axis=1)


def lag_sums(acc):
    rows, width = acc.shape
    rolled = pltpu.roll(acc, 0, 1, stride=1, stride_axis=0)
    sums = jnp.sum(rolled, axis=0, keepdims=True)
    sums = jnp.broadcast_to(sums, (8, width))
    return pltpu.roll(sums, width - rows + 1, 1)[0:1, 0 : width - rows]


def lane_mask(width, nfil, index):
    lane = lax.broadcasted_iota(jnp.int32, (1, width), 1)
    return jnp.where(lane % nfil == index, 1.0, 0.0).astype(jnp.bfloat16)


def second_kernel(half, me_ref, *refs):
    arrived = refs[:half]
    outs = refs[half : 2 * half]
    near_ref, far_ref, line, second_ref, result_ref = refs[2 * half :]
    nfil, size, total = near_ref.shape
    own, width = second_ref.shape
    rows = own // half
    me = me_ref[0]
    fill_bands(half, me, arrived, near_ref, far_ref, line)
    for step in range(half):
        where = rows_at(slot_of(half, me, step), rows)
        second_ref[where, :] = arrived[step][rows : 2 * rows, :]
    masks = [lane_mask(width, nfil, index) for index in range(nfil)]
    for top in range(0, own, size):
        acc = jnp.zeros((size, width), jnp.float32)
        for index in range(nfil):
            acc += jnp.dot(
                far_ref[index, :, own - size - top : own],
                second_ref[0 : top + size, :] * masks[index],
                preferred_element_type=jnp.float32,
            )
        result_ref[top : top + size, :] = acc.astype(jnp.bfloat16)
    for step in range(half):
        outs[step][...] = result_ref[rows_at(slot_of(half, me, step), rows), :]


def inner_kernel(half, me_ref, *refs):
    arrived = refs[:half]
    near_ref, part_ref, flip_ref, lag_ref, first_ref = refs[half:]
    nfil, size, total = near_ref.shape
    own, width = first_ref.shape
    rows = own // half
    me = me_ref[0]
    turn = exchange(rows, True, jnp.bfloat16)
    for step in range(half):
        where = rows_at(slot_of(half, me, step), rows)
        first_ref[where, :] = arrived[step][0:rows, :]
        flip_ref[where, :] = exact_rows(turn, arrived[step][rows : 2 * rows, :])
    masks = [lane_mask(width, nfil, index) for index in range(nfil)]
    for top in range(0, own, size):
        acc = jnp.zeros((size, width), jnp.float32)
        for index in range(nfil):
            acc += jnp.dot(
                near_ref[index, :, 0 : own - top],
                first_ref[top:own, :] * masks[index],
                preferred_element_type=jnp.float32,
            )
        part_ref[top : top + size, :] = acc
    lag_ref[...] = jnp.zeros((8, total), jnp.float32)
    for index in range(nfil):
        acc = jnp.zeros((rows, own + rows), jnp.float32)
        for start in range(0, own, rows):
            acc = add_lags_of(
                first_ref[start:own, :],
                flip_ref[start : start + rows, :],
                masks[index],
                0,
                own + rows,
                acc,
            )
        lag_ref[index : index + 1, 0:own] = lag_sums(acc)


def lag_kernel(half, me_ref, *refs):
    arrived = refs[:half]
    flip_ref, lag_ref, out_ref, first_ref = refs[half:]
    nfil, total = NFILT, lag_ref.shape[1]
    own, width = flip_ref.shape
    rows = own // half
    me = me_ref[0]
    share = width // 2
    lanes = pl.ds(pl.multiple_of(jnp.where(me >= half, share, 0), LANES), share)
    for step in range(half):
        where = rows_at(slot_of(half, me, step), rows)
        first_ref[where, :] = arrived[step][:, lanes]
    out_ref[...] = lag_ref[...]
    for index in range(nfil):
        mask = lane_mask(share, nfil, index)
        acc = jnp.zeros((rows, total + rows), jnp.float32)
        for start in range(0, own, rows):
            acc = add_lags_of(
                first_ref[...],
                flip_ref[start : start + rows, lanes],
                mask,
                own - start,
                total + rows,
                acc,
            )
        out_ref[index : index + 1, :] += lag_sums(acc)


def attach_kernel(half, me_ref, lag_ref, *refs):
    outs, (held, sems) = refs[half : 2 * half], refs[2 * half :]
    rows = outs[0].shape[0] - 16
    nfil = NFILT
    me = me_ref[0]
    copies = []
    for step in range(half):
        pieces = []
        for target in (me ^ step, me ^ step ^ half):
            place = pl.multiple_of(target * LANES, LANES)
            pieces.append(lag_ref[0:nfil, pl.ds(place, LANES)])
        both = jnp.concatenate(pieces, axis=0)
        high = both.astype(jnp.bfloat16).astype(jnp.float32)
        rest = (both - high).astype(jnp.bfloat16).astype(jnp.float32)
        held[step] = jnp.zeros(held.shape[1:], jnp.bfloat16)
        held[step, :, 0:LANES] = jnp.concatenate([high, rest], axis=0).astype(jnp.bfloat16)
        copy = pltpu.make_async_copy(held.at[step], outs[step].at[rows : rows + 16], sems.at[step])
        copy.start()
        copies.append(copy)
    for copy in copies:
        copy.wait()


def outer_kernel(half, me_ref, *refs):
    arrived = refs[:half]
    near_ref, part_ref = refs[half : half + 2]
    outs = refs[half + 2 : 2 * half + 2]
    first_ref, result_ref = refs[2 * half + 2 :]
    nfil, size, total = near_ref.shape
    own, width = part_ref.shape
    rows = own // half
    me = me_ref[0]
    for step in range(half):
        first_ref[rows_at(slot_of(half, me, step), rows), :] = arrived[step][...]
    for top in range(0, own, size):
        acc = part_ref[top : top + size, :]
        for index in range(nfil):
            acc += jnp.dot(
                near_ref[index, :, own - top : total - top],
                first_ref[...] * lane_mask(width, nfil, index),
                preferred_element_type=jnp.float32,
            )
        result_ref[top : top + size, :] = acc.astype(jnp.bfloat16)
    for step in range(half):
        outs[step][0:rows, :] = result_ref[rows_at(slot_of(half, me, step), rows), :]


def final_kernel(half, slim, me_ref, q_ref, k_ref, v_ref, g_ref, *refs):
    firsts, seconds = refs[:half], refs[half : 2 * half]
    outs = refs[2 * half : 2 * half + 4]
    held, sems = refs[2 * half + 4 :]
    rows = q_ref.shape[0]
    me = me_ref[0]
    upper = me >= half
    turn = exchange(rows, upper, jnp.bfloat16)
    copies = []
    for step in range(half):
        part = (me ^ step) & (half - 1)
        lanes = pl.ds(pl.multiple_of(part * slim, LANES), slim)
        first = jnp.dot(turn, firsts[step][0:rows, :], preferred_element_type=jnp.float32)
        second = jnp.dot(turn, seconds[step][...], preferred_element_type=jnp.float32)
        mixed = jnp.where(upper, first, second)
        grad = jnp.where(upper, second, first)
        for index, (ref, value) in enumerate(
            ((q_ref, mixed), (g_ref, mixed), (v_ref, grad), (k_ref, grad))
        ):
            held[step, index] = (ref[:, lanes].astype(jnp.float32) * value).astype(jnp.bfloat16)
            copy = pltpu.make_async_copy(
                held.at[step, index], outs[index].at[:, lanes], sems.at[step, index]
            )
            copy.start()
            copies.append(copy)
    for copy in copies:
        copy.wait()


def swap(value, step, count):
    return lax.ppermute(value, "ctx", [(i, i ^ step) for i in range(count)])


def after(value, *earlier):
    return lax.optimization_barrier((value, *earlier))


def call(kernel, outs, scratch, flops, nbytes, *args, far=0, far_out=False, alias=0):
    near_spec, far_spec = pl.BlockSpec(memory_space=pltpu.VMEM), pl.BlockSpec(memory_space=pl.ANY)
    near = len(args) - 1 - far - alias
    return pl.pallas_call(
        kernel,
        out_shape=outs,
        in_specs=[pl.BlockSpec(memory_space=pltpu.SMEM)]
        + [far_spec] * far
        + [near_spec] * near
        + [far_spec] * alias,
        out_specs=[far_spec if far_out else near_spec] * len(outs),
        scratch_shapes=scratch,
        input_output_aliases={len(args) - alias + k: k for k in range(alias)},
        compiler_params=pltpu.CompilerParams(vmem_limit_bytes=GRANT),
        cost_estimate=pl.CostEstimate(flops=flops, bytes_accessed=nbytes, transcendentals=0),
    )(*args)


def halves_plan(count, chans, queries, keys, values, filters, cotangent):
    rows, width = queries.shape
    nfil = filters.shape[0]
    half = count // 2
    slim = width // half
    total = count * rows
    own = half * rows
    size = min(256, own)
    low = jnp.bfloat16
    shape = jax.ShapeDtypeStruct
    me = lax.axis_index("ctx")
    where = me.astype(jnp.int32).reshape(1)

    taps = jnp.pad(filters.astype(jnp.float32), ((0, 8 - nfil), (0, 0)))
    other_taps = swap(taps, half, count)
    branches = [
        pltpu.with_memory_space_constraint(x, pltpu.HBM)
        for x in (queries, keys, values, cotangent)
    ]
    *sent, pair = call(
        functools.partial(gate_kernel, half, slim),
        [shape((rows, slim), low)] * half + [shape((half, 2, rows, slim), low)],
        [pltpu.VMEM((half, 4, rows, slim), low), pltpu.SemaphoreType.DMA((half, 4))],
        2 * rows * rows * width,
        14 * rows * width,
        where, *branches, far=4,
    )
    inner = call(
        functools.partial(bundle_kernel, half),
        [shape((2 * rows + 16, slim), low)] * half,
        [],
        4 * rows * rows * width,
        8 * rows * width,
        where, taps, other_taps, pair,
    )
    inner = [inner[0]] + [swap(inner[k], k, count) for k in range(1, half)]
    outer = list(sent)
    for k in range(half):
        if k >= half - 2:
            outer[k], inner[k - 1] = after(outer[k], inner[k - 1])
        outer[k] = swap(outer[k], half + k, count)

    *second, near = call(
        functools.partial(second_kernel, half),
        [shape((rows, slim), low)] * half + [shape((nfil, size, total), low)],
        [
            pltpu.VMEM((nfil, size, own), low),
            pltpu.VMEM((8, total), jnp.float32),
            pltpu.VMEM((own, slim), low),
            pltpu.VMEM((own, slim), low),
        ],
        2 * nfil * own * slim * own,
        8 * own * slim,
        where, *inner,
    )
    second = [second[0]] + [swap(second[k], k, count) for k in range(1, half)]
    part, flipped, lags = call(
        functools.partial(inner_kernel, half),
        [
            shape((own, slim), jnp.float32),
            shape((own, slim), low),
            shape((8, total), jnp.float32),
        ],
        [pltpu.VMEM((own, slim), low)],
        4 * nfil * own * slim * own,
        8 * own * slim,
        where, *inner, near,
    )
    (lags,) = call(
        functools.partial(lag_kernel, half),
        [shape((8, total), jnp.float32)],
        [pltpu.VMEM((own, slim // 2), low)],
        nfil * own * slim * own,
        2 * own * slim,
        where, *outer, flipped, lags,
    )
    outer[0], lags = after(outer[0], lags)
    across = lambda value, move, turn: lax.ppermute(
        value,
        ("chan", "ctx"),
        [(c * count + i, (c ^ move) * count + (i ^ turn)) for c in range(chans) for i in range(count)],
    )
    first = call(
        functools.partial(outer_kernel, half),
        [shape((rows + 16, slim), low)] * half,
        [pltpu.VMEM((own, slim), low)] * 2,
        2 * nfil * own * slim * own,
        4 * own * slim,
        where, *outer, near, part,
    )
    lags = lags + across(lags, 1, 0)
    first = call(
        functools.partial(attach_kernel, half),
        [shape((rows + 16, slim), low)] * half,
        [pltpu.VMEM((half, 16, slim), low), pltpu.SemaphoreType.DMA((half,))],
        0,
        32 * slim * half,
        where, lags, *first, alias=half, far_out=True,
    )
    first = [first[0]] + [swap(first[k], k, count) for k in range(1, half)]
    sums = sum(value[rows:, 0:LANES].astype(jnp.float32) for value in first)
    sums = sums[: 2 * nfil] + sums[2 * nfil :]
    mine, other = sums[:nfil], sums[nfil:]
    scale = (total * (D // NFILT)) ** (-0.5)
    arrived = [across(other, 0, half), across(mine, 2, 0), across(other, 2, half)]
    filter_grad = (mine + sum(arrived)) * scale

    outs = call(
        functools.partial(final_kernel, half, slim),
        [shape((rows, width), low)] * 4,
        [pltpu.VMEM((half, 4, rows, slim), low), pltpu.SemaphoreType.DMA((half, 4))],
        4 * rows * rows * width,
        20 * rows * width,
        where, queries, keys, values, cotangent, *first, *second, far_out=True,
    )
    return (*outs, filter_grad)


def toeplitz(padded, base, height, breadth):
    middle = padded.shape[1] // 2
    span = height + breadth - 1
    window = lax.dynamic_slice_in_dim(padded, middle + base - breadth + 1, span, 1)
    flipped = window[:, ::-1]
    tiled = jnp.tile(flipped, (1, height + 1))
    flat = tiled[:, height - 1 : height - 1 + height * (span - 1)]
    return flat.reshape(padded.shape[0], height, span - 1)[:, :, :breadth]


def diagonal_sums(product):
    nfil, height, breadth = product.shape
    stride = height + breadth
    flipped = product[:, :, ::-1]
    padded = jnp.pad(flipped, ((0, 0), (0, 0), (0, height)))
    flat = padded.reshape(nfil, height * stride)[:, : height * (stride - 1)]
    return jnp.sum(flat.reshape(nfil, height, stride - 1), axis=1)


def add_lags(lag_acc, sums, first_lag):
    middle = lag_acc.shape[1] // 2
    where = middle + first_lag
    current = lax.dynamic_slice_in_dim(lag_acc, where, sums.shape[1], 1)
    return lax.dynamic_update_slice_in_dim(lag_acc, current + sums, where, 1)


def channel_plan(queries, keys, values, filters, cotangent):
    rows, width = queries.shape
    nfil = filters.shape[0]
    gated = (keys.astype(jnp.float32) * values.astype(jnp.float32)).astype(jnp.bfloat16)
    back = (cotangent.astype(jnp.float32) * queries.astype(jnp.float32)).astype(jnp.bfloat16)
    taps = lax.all_gather(filters, "ctx", axis=1, tiled=True)
    total = taps.shape[1]
    padded = jnp.concatenate([jnp.zeros_like(taps), taps], axis=1)
    lag_start = jnp.zeros((nfil, 2 * total), jnp.float32)
    chan_gated, chan_back = (
        lax.all_to_all(gated, "ctx", split_axis=1, concat_axis=0, tiled=True),
        lax.all_to_all(back, "ctx", split_axis=1, concat_axis=0, tiled=True),
    )
    blocks = total // rows
    slim = chan_gated.shape[1] // nfil
    gated_cols = chan_gated.reshape(blocks, rows, slim, nfil)
    back_cols = chan_back.reshape(blocks, rows, slim, nfil)
    gated_pad = jnp.concatenate([jnp.zeros_like(gated_cols), gated_cols], axis=0)
    back_pad = jnp.concatenate([back_cols, jnp.zeros_like(back_cols)], axis=0)

    def turn(offset, carry):
        mixed_acc, grad_acc, lag_acc = carry
        tile = toeplitz(padded, offset * rows, rows, rows)
        earlier = lax.dynamic_slice_in_dim(gated_pad, blocks - offset, blocks, 0)
        later = lax.dynamic_slice_in_dim(back_pad, offset, blocks, 0)
        mixed_acc = mixed_acc + jnp.einsum(
            "fst,ntcf->nscf", tile, earlier, preferred_element_type=jnp.float32
        )
        grad_acc = grad_acc + jnp.einsum(
            "fst,nscf->ntcf", tile, later, preferred_element_type=jnp.float32
        )
        product = jnp.einsum(
            "nscf,ntcf->fst", back_cols, earlier, preferred_element_type=jnp.float32
        )
        lag_acc = add_lags(lag_acc, diagonal_sums(product), offset * rows - rows + 1)
        return (mixed_acc, grad_acc, lag_acc)

    blank = jnp.zeros((blocks, rows, slim, nfil), jnp.float32)
    mixed_acc, grad_acc, lag_part = lax.fori_loop(0, blocks, turn, (blank, blank, lag_start))
    mixed_chan = mixed_acc.reshape(total, slim * nfil)
    grad_chan = grad_acc.reshape(total, slim * nfil)
    mixed, gated_grad = (
        lax.all_to_all(mixed_chan, "ctx", split_axis=0, concat_axis=1, tiled=True),
        lax.all_to_all(grad_chan, "ctx", split_axis=0, concat_axis=1, tiled=True),
    )
    lag_share = lax.psum_scatter(
        lag_part[:, total:].astype(jnp.bfloat16), "ctx", scatter_dimension=1, tiled=True
    ).astype(jnp.float32)
    lag_total = lax.psum(lag_share, "chan")
    scale = (total * (D // NFILT)) ** (-0.5)
    filter_grad = lag_total * scale
    output = (queries.astype(jnp.float32) * mixed).astype(jnp.bfloat16)
    query_grad = (cotangent.astype(jnp.float32) * mixed).astype(jnp.bfloat16)
    key_grad = (gated_grad * values.astype(jnp.float32)).astype(jnp.bfloat16)
    value_grad = (gated_grad * keys.astype(jnp.float32)).astype(jnp.bfloat16)
    return (output, query_grad, key_grad, value_grad, filter_grad)


def solution(mesh):
    count, chans = mesh.shape["ctx"], mesh.shape["chan"]

    def shards(queries, keys, values, filters, cotangent):
        width = queries.shape[1]
        quarter = width // max(count // 2, 1)
        if count == 8 and chans == 4 and quarter % (2 * LANES) == 0 and queries.shape[0] == LANES:
            return halves_plan(count, chans, queries, keys, values, filters, cotangent)
        return channel_plan(queries, keys, values, filters, cotangent)

    wide = P("ctx", "chan")
    return jax.shard_map(
        shards,
        mesh=mesh,
        in_specs=(wide, wide, wide, P(None, "ctx"), wide),
        out_specs=(wide, wide, wide, wide, P(None, "ctx")),
        check_vma=False,
    )
```

```python
import functools

import jax
import jax.numpy as jnp
from jax import lax
from jax.experimental import pallas as pl
from jax.experimental.pallas import tpu as pltpu
from jax.sharding import PartitionSpec as P

D = 8192
NFILT = 4
LANES = 128
GRANT = 24 * 2**20


def exchange(size, reverse, dtype):
    row = lax.broadcasted_iota(jnp.int32, (size, size), 0)
    col = lax.broadcasted_iota(jnp.int32, (size, size), 1)
    target = jnp.where(reverse, size - 1 - row, row)
    return jnp.where(col == target, 1.0, 0.0).astype(jnp.float32).astype(dtype)


def exact_rows(matrix, values):
    return jnp.dot(matrix, values, preferred_element_type=jnp.float32).astype(jnp.bfloat16)


def gate_kernel(half, slim, me_ref, q_ref, k_ref, v_ref, g_ref, *refs):
    outs, (pair_ref, held, sems) = refs[:-3], refs[-3:]
    rows = q_ref.shape[0]
    me = me_ref[0]
    upper = me >= half
    copies = []
    for step in range(half):
        part = (me ^ step) & (half - 1)
        lanes = pl.ds(pl.multiple_of(part * slim, LANES), slim)
        copies.append([])
        for index, ref in enumerate((q_ref, k_ref, v_ref, g_ref)):
            copy = pltpu.make_async_copy(
                ref.at[:, lanes], held.at[step, index], sems.at[step, index]
            )
            copy.start()
            copies[step].append(copy)
    turn_other = exchange(rows, jnp.logical_not(upper), jnp.bfloat16)
    for step in range(half):
        for copy in copies[step]:
            copy.wait()
        q, k, v, g = [held[step, index].astype(jnp.float32) for index in range(4)]
        gated = (k * v).astype(jnp.bfloat16)
        back = (g * q).astype(jnp.bfloat16)
        second = jnp.where(upper, back, gated)
        pair_ref[step, 0] = jnp.where(upper, gated, back)
        pair_ref[step, 1] = second
        outs[step][...] = exact_rows(turn_other, second)


def bundle_kernel(half, me_ref, mine_ref, other_ref, pair_ref, *outs):
    rows = pair_ref.shape[2]
    turn = exchange(rows, me_ref[0] >= half, jnp.bfloat16)
    mine, other = mine_ref[...].astype(jnp.float32), other_ref[...].astype(jnp.float32)
    gap = jnp.zeros((8 - mine.shape[0], LANES), jnp.float32)
    both = jnp.concatenate([mine, gap, other, gap], axis=0).astype(jnp.bfloat16)
    for step in range(half):
        outs[step][0:rows, :] = exact_rows(turn, pair_ref[step, 0])
        outs[step][rows : 2 * rows, :] = exact_rows(turn, pair_ref[step, 1])
        outs[step][2 * rows :, :] = jnp.zeros((16, outs[step].shape[1]), jnp.bfloat16)
        outs[step][2 * rows :, 0:LANES] = both


def fill_bands(half, me, arrived, near_ref, far_ref, line):
    nfil, size, total = near_ref.shape
    for step in range(half):
        both = arrived[step][arrived[step].shape[0] - 16 :, 0:LANES].astype(jnp.float32)
        for index, source in enumerate((me ^ step, me ^ step ^ half)):
            place = pl.multiple_of(source * LANES, LANES)
            line[:, pl.ds(place, LANES)] = both[8 * index : 8 * index + 8, :]
    row = lax.broadcasted_iota(jnp.int32, (size, total), 0)
    col = lax.broadcasted_iota(jnp.int32, (size, total), 1)
    reach = far_ref.shape[2] // size
    for index in range(nfil):
        spread = jnp.broadcast_to(line[index : index + 1, :], (size, total))
        rolled = pltpu.roll(spread, 0, 1, stride=1, stride_axis=0)
        band = jnp.where(col >= row, rolled, 0.0)
        near_ref[index] = band.astype(jnp.bfloat16)
        for block in range(reach):
            piece = band[:, (reach - 1 - block) * size : (reach - block) * size]
            far_ref[index, :, block * size : (block + 1) * size] = piece.T.astype(jnp.bfloat16)


def slot_of(half, me, step):
    return ((me ^ step) & (half - 1)) ^ jnp.where(me >= half, half - 1, 0)


def rows_at(slot, rows):
    return pl.ds(pl.multiple_of(slot * rows, rows), rows)


def products(left, right):
    contract = (((1,), (1,)), ((), ()))
    return lax.dot_general(left, right, contract, preferred_element_type=jnp.float32)


def placed(values, start, width):
    rows, reach = values.shape
    pieces = [values, jnp.zeros((rows, width - start - reach), jnp.float32)]
    if start:
        pieces = [jnp.zeros((rows, start), jnp.float32)] + pieces
    return jnp.concatenate(pieces, axis=1)


def diagonal_rows(acc):
    rolled = pltpu.roll(acc, 0, 1, stride=1, stride_axis=0)
    return jnp.broadcast_to(jnp.sum(rolled, axis=0, keepdims=True), (8, acc.shape[1]))


def pair_base(half, me, pair, rows):
    slot = slot_of(half, me, 2 * pair)
    return pl.multiple_of((slot // 2) * 2 * rows, 2 * rows)


def stack_pair(half, me, pair, arrived, target, rows):
    for index in range(2):
        place = (slot_of(half, me, 2 * pair + index) % 2) * rows
        target[pl.ds(pl.multiple_of(place, rows), rows), :] = arrived[index][...]


def outer_lags(half, me, base, pair_ref, flip_ref, lag_ref):
    own, width = flip_ref.shape
    rows = own // half
    reach = pair_ref.shape[0]
    share = width // 2
    window = own + reach
    lanes = pl.ds(pl.multiple_of(jnp.where(me >= half, share, 0), LANES), share)
    for index in range(NFILT):
        right = pair_ref[:, lanes] * lane_mask(share, NFILT, index)
        acc = jnp.zeros((rows, window), jnp.float32)
        for start in range(0, own, rows):
            left = flip_ref[start : start + rows, lanes]
            acc = acc + placed(products(left, right), own - rows - start, window)
        sums = pltpu.roll(diagonal_rows(acc), 1, 1)
        lag_ref[index : index + 1, pl.ds(base, window)] += sums[0:1, :]


def outer_rows(half, top, base, near_ref, pair_ref):
    nfil, size, total = near_ref.shape
    reach, width = pair_ref.shape
    acc = jnp.zeros((size, width), jnp.float32)
    for index in range(nfil):
        start = pl.multiple_of(total // 2 - top + base, reach)
        acc += jnp.dot(
            near_ref[index, :, pl.ds(start, reach)],
            pair_ref[...] * lane_mask(width, nfil, index),
            preferred_element_type=jnp.float32,
        )
    return acc


def lane_mask(width, nfil, index):
    lane = lax.broadcasted_iota(jnp.int32, (1, width), 1)
    return jnp.where(lane % nfil == index, 1.0, 0.0).astype(jnp.bfloat16)


def inner_kernel(half, me_ref, *refs):
    arrived, across = refs[:half], refs[half : half + 2]
    outs = refs[half + 2 : 2 * half + 2]
    near_ref, part_ref, flip_ref, lag_ref = refs[2 * half + 2 : 2 * half + 6]
    far_ref, line, first_ref, second_ref, pair_ref, result_ref = refs[2 * half + 6 :]
    nfil, size, total = near_ref.shape
    own, width = second_ref.shape
    rows = own // half
    me = me_ref[0]
    turn = exchange(rows, True, jnp.bfloat16)
    fill_bands(half, me, arrived, near_ref, far_ref, line)
    for step in range(half):
        where = rows_at(slot_of(half, me, step), rows)
        first_ref[where, :] = arrived[step][0:rows, :]
        second_ref[where, :] = arrived[step][rows : 2 * rows, :]
        flip_ref[where, :] = exact_rows(turn, arrived[step][rows : 2 * rows, :])
    stack_pair(half, me, 0, across, pair_ref, rows)
    base = pair_base(half, me, 0, rows)
    masks = [lane_mask(width, nfil, index) for index in range(nfil)]
    for top in range(0, own, size):
        acc = jnp.zeros((size, width), jnp.float32)
        for index in range(nfil):
            acc += jnp.dot(
                far_ref[index, :, own - size - top : own],
                second_ref[0 : top + size, :] * masks[index],
                preferred_element_type=jnp.float32,
            )
        result_ref[top : top + size, :] = acc.astype(jnp.bfloat16)
    for step in range(half):
        outs[step][...] = result_ref[rows_at(slot_of(half, me, step), rows), :]
    for top in range(0, own, size):
        acc = outer_rows(half, top, base, near_ref, pair_ref)
        for index in range(nfil):
            acc += jnp.dot(
                near_ref[index, :, 0 : own - top],
                first_ref[top:own, :] * masks[index],
                preferred_element_type=jnp.float32,
            )
        part_ref[top : top + size, :] = acc
    lag_ref[...] = jnp.zeros((8, total), jnp.float32)
    for index in range(nfil):
        acc = jnp.zeros((rows, own + rows), jnp.float32)
        for start in range(0, own, rows):
            right = first_ref[start:own, :] * masks[index]
            acc = acc + placed(
                products(flip_ref[start : start + rows, :], right), 0, own + rows
            )
        sums = pltpu.roll(diagonal_rows(acc), own + 1, 1)
        lag_ref[index : index + 1, 0:own] = sums[0:1, 0:own]
    outer_lags(half, me, base, pair_ref, flip_ref, lag_ref)


def lag_kernel(half, me_ref, *refs):
    across = refs[:2]
    flip_ref, lag_ref, out_ref, pair_ref = refs[2:]
    rows = flip_ref.shape[0] // half
    me = me_ref[0]
    stack_pair(half, me, 1, across, pair_ref, rows)
    out_ref[...] = lag_ref[...]
    outer_lags(half, me, pair_base(half, me, 1, rows), pair_ref, flip_ref, out_ref)


def attach_kernel(half, me_ref, lag_ref, *refs):
    outs, (held, sems) = refs[half : 2 * half], refs[2 * half :]
    rows = outs[0].shape[0] - 16
    nfil = NFILT
    me = me_ref[0]
    copies = []
    for step in range(half):
        pieces = []
        for target in (me ^ step, me ^ step ^ half):
            place = pl.multiple_of(target * LANES, LANES)
            pieces.append(lag_ref[0:nfil, pl.ds(place, LANES)])
        both = jnp.concatenate(pieces, axis=0)
        high = both.astype(jnp.bfloat16).astype(jnp.float32)
        rest = (both - high).astype(jnp.bfloat16).astype(jnp.float32)
        held[step] = jnp.zeros(held.shape[1:], jnp.bfloat16)
        held[step, :, 0:LANES] = jnp.concatenate([high, rest], axis=0).astype(jnp.bfloat16)
        copy = pltpu.make_async_copy(held.at[step], outs[step].at[rows : rows + 16], sems.at[step])
        copy.start()
        copies.append(copy)
    for copy in copies:
        copy.wait()


def outer_kernel(half, me_ref, *refs):
    across = refs[:2]
    near_ref, part_ref = refs[2:4]
    outs = refs[4 : half + 4]
    pair_ref, result_ref = refs[half + 4 :]
    nfil, size, total = near_ref.shape
    own, width = part_ref.shape
    rows = own // half
    me = me_ref[0]
    stack_pair(half, me, 1, across, pair_ref, rows)
    base = pair_base(half, me, 1, rows)
    for top in range(0, own, size):
        acc = part_ref[top : top + size, :] + outer_rows(half, top, base, near_ref, pair_ref)
        result_ref[top : top + size, :] = acc.astype(jnp.bfloat16)
    for step in range(half):
        outs[step][0:rows, :] = result_ref[rows_at(slot_of(half, me, step), rows), :]


def final_kernel(half, slim, me_ref, q_ref, k_ref, v_ref, g_ref, *refs):
    firsts, seconds = refs[:half], refs[half : 2 * half]
    outs = refs[2 * half : 2 * half + 4]
    held, sems = refs[2 * half + 4 :]
    rows = q_ref.shape[0]
    me = me_ref[0]
    upper = me >= half
    turn = exchange(rows, upper, jnp.bfloat16)
    copies = []
    for step in range(half):
        part = (me ^ step) & (half - 1)
        lanes = pl.ds(pl.multiple_of(part * slim, LANES), slim)
        first = jnp.dot(turn, firsts[step][0:rows, :], preferred_element_type=jnp.float32)
        second = jnp.dot(turn, seconds[step][...], preferred_element_type=jnp.float32)
        mixed = jnp.where(upper, first, second)
        grad = jnp.where(upper, second, first)
        for index, (ref, value) in enumerate(
            ((q_ref, mixed), (g_ref, mixed), (v_ref, grad), (k_ref, grad))
        ):
            held[step, index] = (ref[:, lanes].astype(jnp.float32) * value).astype(jnp.bfloat16)
            copy = pltpu.make_async_copy(
                held.at[step, index], outs[index].at[:, lanes], sems.at[step, index]
            )
            copy.start()
            copies.append(copy)
    for copy in copies:
        copy.wait()


def swap(value, step, count):
    return lax.ppermute(value, "ctx", [(i, i ^ step) for i in range(count)])


def after(value, *earlier):
    return lax.optimization_barrier((value, *earlier))


def call(kernel, outs, scratch, flops, nbytes, *args, far=0, far_out=False, alias=0):
    near_spec, far_spec = pl.BlockSpec(memory_space=pltpu.VMEM), pl.BlockSpec(memory_space=pl.ANY)
    near = len(args) - 1 - far - alias
    return pl.pallas_call(
        kernel,
        out_shape=outs,
        in_specs=[pl.BlockSpec(memory_space=pltpu.SMEM)]
        + [far_spec] * far
        + [near_spec] * near
        + [far_spec] * alias,
        out_specs=[far_spec if far_out else near_spec] * len(outs),
        scratch_shapes=scratch,
        input_output_aliases={len(args) - alias + k: k for k in range(alias)},
        compiler_params=pltpu.CompilerParams(vmem_limit_bytes=GRANT),
        cost_estimate=pl.CostEstimate(flops=flops, bytes_accessed=nbytes, transcendentals=0),
    )(*args)


def halves_plan(count, chans, queries, keys, values, filters, cotangent):
    rows, width = queries.shape
    nfil = filters.shape[0]
    half = count // 2
    slim = width // half
    total = count * rows
    own = half * rows
    size = min(256, own)
    low = jnp.bfloat16
    shape = jax.ShapeDtypeStruct
    me = lax.axis_index("ctx")
    where = me.astype(jnp.int32).reshape(1)

    other_taps = swap(filters, half, count)
    branches = [
        pltpu.with_memory_space_constraint(x, pltpu.HBM)
        for x in (queries, keys, values, cotangent)
    ]
    *sent, pair = call(
        functools.partial(gate_kernel, half, slim),
        [shape((rows, slim), low)] * half + [shape((half, 2, rows, slim), low)],
        [pltpu.VMEM((half, 4, rows, slim), low), pltpu.SemaphoreType.DMA((half, 4))],
        2 * rows * rows * width,
        14 * rows * width,
        where, *branches, far=4,
    )
    inner = call(
        functools.partial(bundle_kernel, half),
        [shape((2 * rows + 16, slim), low)] * half,
        [],
        4 * rows * rows * width,
        8 * rows * width,
        where, filters, other_taps, pair,
    )
    inner = [inner[0]] + [swap(inner[k], k, count) for k in range(1, half)]
    outer = list(sent)
    outer[0] = swap(outer[0], half, count)
    outer[1] = swap(outer[1], half + 1, count)
    outer[2], inner[1] = after(outer[2], inner[1])
    outer[2] = swap(outer[2], half + 2, count)
    outer[3], inner[2] = after(outer[3], inner[2])
    outer[3] = swap(outer[3], half + 3, count)

    *second, near, part, flipped, lags = call(
        functools.partial(inner_kernel, half),
        [shape((rows, slim), low)] * half
        + [
            shape((nfil, size, total), low),
            shape((own, slim), jnp.float32),
            shape((own, slim), low),
            shape((8, total), jnp.float32),
        ],
        [
            pltpu.VMEM((nfil, size, own), low),
            pltpu.VMEM((8, total), jnp.float32),
            pltpu.VMEM((own, slim), low),
            pltpu.VMEM((own, slim), low),
            pltpu.VMEM((2 * rows, slim), low),
            pltpu.VMEM((own, slim), low),
        ],
        8 * nfil * own * slim * own,
        8 * own * slim,
        where, *inner, *outer[:2],
    )
    second = [second[0]] + [swap(second[k], k, count) for k in range(1, half)]
    across = lambda value, move, turn: lax.ppermute(
        value,
        ("chan", "ctx"),
        [(c * count + i, (c ^ move) * count + (i ^ turn)) for c in range(chans) for i in range(count)],
    )
    (lags,) = call(
        functools.partial(lag_kernel, half),
        [shape((8, total), jnp.float32)],
        [pltpu.VMEM((2 * rows, slim), low)],
        nfil * own * slim * own // 2,
        own * slim,
        where, *outer[2:], flipped, lags,
    )
    outer[2], lags = after(outer[2], lags)
    first = call(
        functools.partial(outer_kernel, half),
        [shape((rows + 16, slim), low)] * half,
        [pltpu.VMEM((2 * rows, slim), low), pltpu.VMEM((own, slim), low)],
        nfil * own * slim * own,
        4 * own * slim,
        where, *outer[2:], near, part,
    )
    lags = lags + across(lags, 1, 0)
    first = call(
        functools.partial(attach_kernel, half),
        [shape((rows + 16, slim), low)] * half,
        [pltpu.VMEM((half, 16, slim), low), pltpu.SemaphoreType.DMA((half,))],
        0,
        32 * slim * half,
        where, lags, *first, alias=half, far_out=True,
    )
    first = [first[0]] + [swap(first[k], k, count) for k in range(1, half)]
    sums = sum(value[rows:, 0:LANES].astype(jnp.float32) for value in first)
    sums = sums[: 2 * nfil] + sums[2 * nfil :]
    mine, other = sums[:nfil], sums[nfil:]
    scale = (total * (D // NFILT)) ** (-0.5)
    arrived = [across(other, 0, half), across(mine, 2, 0), across(other, 2, half)]
    filter_grad = (mine + sum(arrived)) * scale

    outs = call(
        functools.partial(final_kernel, half, slim),
        [shape((rows, width), low)] * 4,
        [pltpu.VMEM((half, 4, rows, slim), low), pltpu.SemaphoreType.DMA((half, 4))],
        4 * rows * rows * width,
        20 * rows * width,
        where, queries, keys, values, cotangent, *first, *second, far_out=True,
    )
    return (*outs, filter_grad)


def toeplitz(padded, base, height, breadth):
    middle = padded.shape[1] // 2
    span = height + breadth - 1
    window = lax.dynamic_slice_in_dim(padded, middle + base - breadth + 1, span, 1)
    flipped = window[:, ::-1]
    tiled = jnp.tile(flipped, (1, height + 1))
    flat = tiled[:, height - 1 : height - 1 + height * (span - 1)]
    return flat.reshape(padded.shape[0], height, span - 1)[:, :, :breadth]


def diagonal_sums(product):
    nfil, height, breadth = product.shape
    stride = height + breadth
    flipped = product[:, :, ::-1]
    padded = jnp.pad(flipped, ((0, 0), (0, 0), (0, height)))
    flat = padded.reshape(nfil, height * stride)[:, : height * (stride - 1)]
    return jnp.sum(flat.reshape(nfil, height, stride - 1), axis=1)


def add_lags(lag_acc, sums, first_lag):
    middle = lag_acc.shape[1] // 2
    where = middle + first_lag
    current = lax.dynamic_slice_in_dim(lag_acc, where, sums.shape[1], 1)
    return lax.dynamic_update_slice_in_dim(lag_acc, current + sums, where, 1)


def channel_plan(queries, keys, values, filters, cotangent):
    rows, width = queries.shape
    nfil = filters.shape[0]
    gated = (keys.astype(jnp.float32) * values.astype(jnp.float32)).astype(jnp.bfloat16)
    back = (cotangent.astype(jnp.float32) * queries.astype(jnp.float32)).astype(jnp.bfloat16)
    taps = lax.all_gather(filters, "ctx", axis=1, tiled=True)
    total = taps.shape[1]
    padded = jnp.concatenate([jnp.zeros_like(taps), taps], axis=1)
    lag_start = jnp.zeros((nfil, 2 * total), jnp.float32)
    chan_gated, chan_back = (
        lax.all_to_all(gated, "ctx", split_axis=1, concat_axis=0, tiled=True),
        lax.all_to_all(back, "ctx", split_axis=1, concat_axis=0, tiled=True),
    )
    blocks = total // rows
    slim = chan_gated.shape[1] // nfil
    gated_cols = chan_gated.reshape(blocks, rows, slim, nfil)
    back_cols = chan_back.reshape(blocks, rows, slim, nfil)
    gated_pad = jnp.concatenate([jnp.zeros_like(gated_cols), gated_cols], axis=0)
    back_pad = jnp.concatenate([back_cols, jnp.zeros_like(back_cols)], axis=0)

    def turn(offset, carry):
        mixed_acc, grad_acc, lag_acc = carry
        tile = toeplitz(padded, offset * rows, rows, rows)
        earlier = lax.dynamic_slice_in_dim(gated_pad, blocks - offset, blocks, 0)
        later = lax.dynamic_slice_in_dim(back_pad, offset, blocks, 0)
        mixed_acc = mixed_acc + jnp.einsum(
            "fst,ntcf->nscf", tile, earlier, preferred_element_type=jnp.float32
        )
        grad_acc = grad_acc + jnp.einsum(
            "fst,nscf->ntcf", tile, later, preferred_element_type=jnp.float32
        )
        product = jnp.einsum(
            "nscf,ntcf->fst", back_cols, earlier, preferred_element_type=jnp.float32
        )
        lag_acc = add_lags(lag_acc, diagonal_sums(product), offset * rows - rows + 1)
        return (mixed_acc, grad_acc, lag_acc)

    blank = jnp.zeros((blocks, rows, slim, nfil), jnp.float32)
    mixed_acc, grad_acc, lag_part = lax.fori_loop(0, blocks, turn, (blank, blank, lag_start))
    mixed_chan = mixed_acc.reshape(total, slim * nfil)
    grad_chan = grad_acc.reshape(total, slim * nfil)
    mixed, gated_grad = (
        lax.all_to_all(mixed_chan, "ctx", split_axis=0, concat_axis=1, tiled=True),
        lax.all_to_all(grad_chan, "ctx", split_axis=0, concat_axis=1, tiled=True),
    )
    lag_share = lax.psum_scatter(
        lag_part[:, total:].astype(jnp.bfloat16), "ctx", scatter_dimension=1, tiled=True
    ).astype(jnp.float32)
    lag_total = lax.psum(lag_share, "chan")
    scale = (total * (D // NFILT)) ** (-0.5)
    filter_grad = lag_total * scale
    output = (queries.astype(jnp.float32) * mixed).astype(jnp.bfloat16)
    query_grad = (cotangent.astype(jnp.float32) * mixed).astype(jnp.bfloat16)
    key_grad = (gated_grad * values.astype(jnp.float32)).astype(jnp.bfloat16)
    value_grad = (gated_grad * keys.astype(jnp.float32)).astype(jnp.bfloat16)
    return (output, query_grad, key_grad, value_grad, filter_grad)


def solution(mesh):
    count, chans = mesh.shape["ctx"], mesh.shape["chan"]

    def shards(queries, keys, values, filters, cotangent):
        width = queries.shape[1]
        quarter = width // max(count // 2, 1)
        if count == 8 and chans == 4 and quarter % (2 * LANES) == 0 and queries.shape[0] == LANES:
            return halves_plan(count, chans, queries, keys, values, filters, cotangent)
        return channel_plan(queries, keys, values, filters, cotangent)

    wide = P("ctx", "chan")
    return jax.shard_map(
        shards,
        mesh=mesh,
        in_specs=(wide, wide, wide, P(None, "ctx"), wide),
        out_specs=(wide, wide, wide, wide, P(None, "ctx")),
        check_vma=False,
    )
```

```python
import functools

import jax
import jax.numpy as jnp
from jax import lax
from jax.experimental import pallas as pl
from jax.experimental.pallas import tpu as pltpu
from jax.sharding import PartitionSpec as P

D = 8192
NFILT = 4
LANES = 128
GRANT = 24 * 2**20


def exchange(size, reverse, dtype):
    row = lax.broadcasted_iota(jnp.int32, (size, size), 0)
    col = lax.broadcasted_iota(jnp.int32, (size, size), 1)
    target = jnp.where(reverse, size - 1 - row, row)
    return jnp.where(col == target, 1.0, 0.0).astype(jnp.float32).astype(dtype)


def exact_rows(matrix, values):
    return jnp.dot(matrix, values, preferred_element_type=jnp.float32).astype(jnp.bfloat16)


def gate_kernel(half, slim, me_ref, q_ref, k_ref, v_ref, g_ref, *refs):
    outs, (pair_ref, held, sems) = refs[:-3], refs[-3:]
    rows = q_ref.shape[0]
    me = me_ref[0]
    upper = me >= half
    copies = []
    for chunk in range(half // 2):
        base = (((me & (half - 1)) // 2) ^ chunk) * 2 * slim
        lanes = pl.ds(pl.multiple_of(base, LANES), 2 * slim)
        copies.append([])
        for index, ref in enumerate((q_ref, k_ref, v_ref, g_ref)):
            copy = pltpu.make_async_copy(
                ref.at[:, lanes], held.at[chunk, index], sems.at[chunk, index]
            )
            copy.start()
            copies[chunk].append(copy)
    turn_other = exchange(rows, jnp.logical_not(upper), jnp.bfloat16)
    for step in range(half):
        if step % 2 == 0:
            for copy in copies[step // 2]:
                copy.wait()
        lanes = pl.ds(pl.multiple_of(((me ^ step) & 1) * slim, LANES), slim)
        q, k, v, g = [held[step // 2, index, :, lanes].astype(jnp.float32) for index in range(4)]
        gated = (k * v).astype(jnp.bfloat16)
        back = (g * q).astype(jnp.bfloat16)
        second = jnp.where(upper, back, gated)
        pair_ref[step, 0] = jnp.where(upper, gated, back)
        pair_ref[step, 1] = second
        outs[step][...] = exact_rows(turn_other, second)


def bundle_kernel(half, me_ref, mine_ref, other_ref, pair_ref, *outs):
    rows = pair_ref.shape[2]
    turn = exchange(rows, me_ref[0] >= half, jnp.bfloat16)
    mine, other = mine_ref[...].astype(jnp.float32), other_ref[...].astype(jnp.float32)
    gap = jnp.zeros((8 - mine.shape[0], LANES), jnp.float32)
    both = jnp.concatenate([mine, gap, other, gap], axis=0).astype(jnp.bfloat16)
    for step in range(half):
        outs[step][0:rows, :] = exact_rows(turn, pair_ref[step, 0])
        outs[step][rows : 2 * rows, :] = exact_rows(turn, pair_ref[step, 1])
        outs[step][2 * rows :, :] = jnp.zeros((16, outs[step].shape[1]), jnp.bfloat16)
        outs[step][2 * rows :, 0:LANES] = both


def fill_bands(half, me, arrived, near_ref, far_ref, line):
    nfil, size, total = near_ref.shape
    for step in range(half):
        both = arrived[step][arrived[step].shape[0] - 16 :, 0:LANES].astype(jnp.float32)
        for index, source in enumerate((me ^ step, me ^ step ^ half)):
            place = pl.multiple_of(source * LANES, LANES)
            line[:, pl.ds(place, LANES)] = both[8 * index : 8 * index + 8, :]
    row = lax.broadcasted_iota(jnp.int32, (size, total), 0)
    col = lax.broadcasted_iota(jnp.int32, (size, total), 1)
    reach = far_ref.shape[2] // size
    for index in range(nfil):
        spread = jnp.broadcast_to(line[index : index + 1, :], (size, total))
        rolled = pltpu.roll(spread, 0, 1, stride=1, stride_axis=0)
        band = jnp.where(col >= row, rolled, 0.0)
        near_ref[index] = band.astype(jnp.bfloat16)
        for block in range(reach):
            piece = band[:, (reach - 1 - block) * size : (reach - block) * size]
            far_ref[index, :, block * size : (block + 1) * size] = piece.T.astype(jnp.bfloat16)


def slot_of(half, me, step):
    return ((me ^ step) & (half - 1)) ^ jnp.where(me >= half, half - 1, 0)


def rows_at(slot, rows):
    return pl.ds(pl.multiple_of(slot * rows, rows), rows)


def products(left, right):
    contract = (((1,), (1,)), ((), ()))
    return lax.dot_general(left, right, contract, preferred_element_type=jnp.float32)


def add_columns(columns, values, start):
    first = start // LANES
    for index in range(values.shape[1] // LANES):
        piece = values[:, index * LANES : (index + 1) * LANES]
        have = columns[first + index]
        columns[first + index] = piece if have is None else have + piece


def joined_columns(columns, rows):
    blank = jnp.zeros((rows, LANES), jnp.float32)
    return jnp.concatenate([blank if c is None else c for c in columns], axis=1)


def diagonal_rows(acc):
    rolled = pltpu.roll(acc, 0, 1, stride=1, stride_axis=0)
    return jnp.broadcast_to(jnp.sum(rolled, axis=0, keepdims=True), (8, acc.shape[1]))


def pair_base(half, me, pair, rows):
    slot = slot_of(half, me, 2 * pair)
    return pl.multiple_of((slot // 2) * 2 * rows, 2 * rows)


def stack_pair(half, me, pair, arrived, target, rows):
    for index in range(2):
        place = (slot_of(half, me, 2 * pair + index) % 2) * rows
        target[pl.ds(pl.multiple_of(place, rows), rows), :] = arrived[index][...]


def outer_lags(half, me, base, pair_ref, flip_ref, lag_ref):
    own, width = flip_ref.shape
    rows = own // half
    reach = pair_ref.shape[0]
    share = width // 2
    window = own + reach
    lanes = pl.ds(pl.multiple_of(jnp.where(me >= half, share, 0), LANES), share)
    for index in range(NFILT):
        right = pair_ref[:, lanes] * lane_mask(share, NFILT, index)
        columns = [None] * (window // LANES)
        every = products(flip_ref[:, lanes], right)
        for start in range(0, own, rows):
            add_columns(columns, every[start : start + rows, :], own - rows - start)
        sums = pltpu.roll(diagonal_rows(joined_columns(columns, rows)), 1, 1)
        lag_ref[index : index + 1, pl.ds(base, window)] += sums[0:1, :]


def outer_rows(half, top, base, near_ref, pair_ref):
    nfil, size, total = near_ref.shape
    reach, width = pair_ref.shape
    acc = jnp.zeros((size, width), jnp.float32)
    for index in range(nfil):
        start = pl.multiple_of(total // 2 - top + base, reach)
        acc += jnp.dot(
            near_ref[index, :, pl.ds(start, reach)],
            pair_ref[...] * lane_mask(width, nfil, index),
            preferred_element_type=jnp.float32,
        )
    return acc


def lane_mask(width, nfil, index):
    lane = lax.broadcasted_iota(jnp.int32, (1, width), 1)
    return jnp.where(lane % nfil == index, 1.0, 0.0).astype(jnp.bfloat16)


def inner_kernel(half, me_ref, *refs):
    arrived, across = refs[:half], refs[half : half + 2]
    outs = refs[half + 2 : 2 * half + 2]
    near_ref, part_ref, flip_ref, lag_ref = refs[2 * half + 2 : 2 * half + 6]
    far_ref, line, first_ref, second_ref, pair_ref, result_ref = refs[2 * half + 6 :]
    nfil, size, total = near_ref.shape
    own, width = second_ref.shape
    rows = own // half
    me = me_ref[0]
    turn = exchange(rows, True, jnp.bfloat16)
    fill_bands(half, me, arrived, near_ref, far_ref, line)
    for step in range(half):
        where = rows_at(slot_of(half, me, step), rows)
        first_ref[where, :] = arrived[step][0:rows, :]
        second_ref[where, :] = arrived[step][rows : 2 * rows, :]
        flip_ref[where, :] = exact_rows(turn, arrived[step][rows : 2 * rows, :])
    stack_pair(half, me, 0, across, pair_ref, rows)
    base = pair_base(half, me, 0, rows)
    masks = [lane_mask(width, nfil, index) for index in range(nfil)]
    for top in range(0, own, size):
        acc = jnp.zeros((size, width), jnp.float32)
        for index in range(nfil):
            acc += jnp.dot(
                far_ref[index, :, own - size - top : own],
                second_ref[0 : top + size, :] * masks[index],
                preferred_element_type=jnp.float32,
            )
        result_ref[top : top + size, :] = acc.astype(jnp.bfloat16)
    for step in range(half):
        outs[step][...] = result_ref[rows_at(slot_of(half, me, step), rows), :]
    for top in range(0, own, size):
        acc = outer_rows(half, top, base, near_ref, pair_ref)
        for index in range(nfil):
            acc += jnp.dot(
                near_ref[index, :, 0 : own - top],
                first_ref[top:own, :] * masks[index],
                preferred_element_type=jnp.float32,
            )
        part_ref[top : top + size, :] = acc
    lag_ref[...] = jnp.zeros((8, total), jnp.float32)
    for index in range(nfil):
        columns = [None] * ((own + rows) // LANES)
        every = products(flip_ref[...], first_ref[...] * masks[index])
        for start in range(0, own, rows):
            add_columns(columns, every[start : start + rows, start:own], 0)
        sums = pltpu.roll(diagonal_rows(joined_columns(columns, rows)), own + 1, 1)
        lag_ref[index : index + 1, 0:own] = sums[0:1, 0:own]
    outer_lags(half, me, base, pair_ref, flip_ref, lag_ref)


def lag_kernel(half, me_ref, *refs):
    across = refs[:2]
    flip_ref, lag_ref, out_ref, pair_ref = refs[2:]
    rows = flip_ref.shape[0] // half
    me = me_ref[0]
    stack_pair(half, me, 1, across, pair_ref, rows)
    out_ref[...] = lag_ref[...]
    outer_lags(half, me, pair_base(half, me, 1, rows), pair_ref, flip_ref, out_ref)


def attach_kernel(half, me_ref, lag_ref, *refs):
    outs, (held, sems) = refs[half : 2 * half], refs[2 * half :]
    rows = outs[0].shape[0] - 16
    nfil = NFILT
    me = me_ref[0]
    copies = []
    for step in range(half):
        pieces = []
        for target in (me ^ step, me ^ step ^ half):
            place = pl.multiple_of(target * LANES, LANES)
            pieces.append(lag_ref[0:nfil, pl.ds(place, LANES)])
        both = jnp.concatenate(pieces, axis=0)
        high = both.astype(jnp.bfloat16).astype(jnp.float32)
        rest = (both - high).astype(jnp.bfloat16).astype(jnp.float32)
        held[step] = jnp.zeros(held.shape[1:], jnp.bfloat16)
        held[step, :, 0:LANES] = jnp.concatenate([high, rest], axis=0).astype(jnp.bfloat16)
        copy = pltpu.make_async_copy(held.at[step], outs[step].at[rows : rows + 16], sems.at[step])
        copy.start()
        copies.append(copy)
    for copy in copies:
        copy.wait()


def outer_kernel(half, me_ref, *refs):
    across = refs[:2]
    near_ref, part_ref = refs[2:4]
    outs = refs[4 : half + 4]
    pair_ref, result_ref = refs[half + 4 :]
    nfil, size, total = near_ref.shape
    own, width = part_ref.shape
    rows = own // half
    me = me_ref[0]
    stack_pair(half, me, 1, across, pair_ref, rows)
    base = pair_base(half, me, 1, rows)
    for top in range(0, own, size):
        acc = part_ref[top : top + size, :] + outer_rows(half, top, base, near_ref, pair_ref)
        result_ref[top : top + size, :] = acc.astype(jnp.bfloat16)
    for step in range(half):
        outs[step][0:rows, :] = result_ref[rows_at(slot_of(half, me, step), rows), :]


def final_kernel(half, slim, me_ref, q_ref, k_ref, v_ref, g_ref, *refs):
    firsts, seconds = refs[:half], refs[half : 2 * half]
    outs = refs[2 * half : 2 * half + 4]
    held, sems = refs[2 * half + 4 :]
    rows = q_ref.shape[0]
    me = me_ref[0]
    upper = me >= half
    turn = exchange(rows, upper, jnp.bfloat16)
    copies = []
    for step in range(half):
        part = (me ^ step) & (half - 1)
        lanes = pl.ds(pl.multiple_of(part * slim, LANES), slim)
        first = jnp.dot(turn, firsts[step][0:rows, :], preferred_element_type=jnp.float32)
        second = jnp.dot(turn, seconds[step][...], preferred_element_type=jnp.float32)
        mixed = jnp.where(upper, first, second)
        grad = jnp.where(upper, second, first)
        for index, (ref, value) in enumerate(
            ((q_ref, mixed), (g_ref, mixed), (v_ref, grad), (k_ref, grad))
        ):
            held[step, index] = (ref[:, lanes].astype(jnp.float32) * value).astype(jnp.bfloat16)
            copy = pltpu.make_async_copy(
                held.at[step, index], outs[index].at[:, lanes], sems.at[step, index]
            )
            copy.start()
            copies.append(copy)
    for copy in copies:
        copy.wait()


def swap(value, step, count):
    return lax.ppermute(value, "ctx", [(i, i ^ step) for i in range(count)])


def after(value, *earlier):
    return lax.optimization_barrier((value, *earlier))


def call(kernel, outs, scratch, flops, nbytes, *args, far=0, far_out=False, alias=0):
    near_spec, far_spec = pl.BlockSpec(memory_space=pltpu.VMEM), pl.BlockSpec(memory_space=pl.ANY)
    near = len(args) - 1 - far - alias
    return pl.pallas_call(
        kernel,
        out_shape=outs,
        in_specs=[pl.BlockSpec(memory_space=pltpu.SMEM)]
        + [far_spec] * far
        + [near_spec] * near
        + [far_spec] * alias,
        out_specs=[far_spec if far_out else near_spec] * len(outs),
        scratch_shapes=scratch,
        input_output_aliases={len(args) - alias + k: k for k in range(alias)},
        compiler_params=pltpu.CompilerParams(vmem_limit_bytes=GRANT),
        cost_estimate=pl.CostEstimate(flops=flops, bytes_accessed=nbytes, transcendentals=0),
    )(*args)


def halves_plan(count, chans, queries, keys, values, filters, cotangent):
    rows, width = queries.shape
    nfil = filters.shape[0]
    half = count // 2
    slim = width // half
    total = count * rows
    own = half * rows
    size = min(256, own)
    low = jnp.bfloat16
    shape = jax.ShapeDtypeStruct
    me = lax.axis_index("ctx")
    where = me.astype(jnp.int32).reshape(1)

    other_taps = swap(filters, half, count)
    branches = [
        pltpu.with_memory_space_constraint(x, pltpu.HBM)
        for x in (queries, keys, values, cotangent)
    ]
    *sent, pair = call(
        functools.partial(gate_kernel, half, slim),
        [shape((rows, slim), low)] * half + [shape((half, 2, rows, slim), low)],
        [pltpu.VMEM((half // 2, 4, rows, 2 * slim), low), pltpu.SemaphoreType.DMA((half // 2, 4))],
        2 * rows * rows * width,
        14 * rows * width,
        where, *branches, far=4,
    )
    inner = call(
        functools.partial(bundle_kernel, half),
        [shape((2 * rows + 16, slim), low)] * half,
        [],
        4 * rows * rows * width,
        8 * rows * width,
        where, filters, other_taps, pair,
    )
    inner = [inner[0]] + [swap(inner[k], k, count) for k in range(1, half)]
    outer = list(sent)
    outer[0] = swap(outer[0], half, count)
    outer[1] = swap(outer[1], half + 1, count)
    outer[2], inner[1] = after(outer[2], inner[1])
    outer[2] = swap(outer[2], half + 2, count)
    outer[3], inner[2] = after(outer[3], inner[2])
    outer[3] = swap(outer[3], half + 3, count)

    *second, near, part, flipped, lags = call(
        functools.partial(inner_kernel, half),
        [shape((rows, slim), low)] * half
        + [
            shape((nfil, size, total), low),
            shape((own, slim), jnp.float32),
            shape((own, slim), low),
            shape((8, total), jnp.float32),
        ],
        [
            pltpu.VMEM((nfil, size, own), low),
            pltpu.VMEM((8, total), jnp.float32),
            pltpu.VMEM((own, slim), low),
            pltpu.VMEM((own, slim), low),
            pltpu.VMEM((2 * rows, slim), low),
            pltpu.VMEM((own, slim), low),
        ],
        8 * nfil * own * slim * own,
        8 * own * slim,
        where, *inner, *outer[:2],
    )
    second = [second[0]] + [swap(second[k], k, count) for k in range(1, half)]
    across = lambda value, move, turn: lax.ppermute(
        value,
        ("chan", "ctx"),
        [(c * count + i, (c ^ move) * count + (i ^ turn)) for c in range(chans) for i in range(count)],
    )
    (lags,) = call(
        functools.partial(lag_kernel, half),
        [shape((8, total), jnp.float32)],
        [pltpu.VMEM((2 * rows, slim), low)],
        nfil * own * slim * own // 2,
        own * slim,
        where, *outer[2:], flipped, lags,
    )
    outer[2], lags = after(outer[2], lags)
    first = call(
        functools.partial(outer_kernel, half),
        [shape((rows + 16, slim), low)] * half,
        [pltpu.VMEM((2 * rows, slim), low), pltpu.VMEM((own, slim), low)],
        nfil * own * slim * own,
        4 * own * slim,
        where, *outer[2:], near, part,
    )
    lags = lags + across(lags, 1, 0)
    first = call(
        functools.partial(attach_kernel, half),
        [shape((rows + 16, slim), low)] * half,
        [pltpu.VMEM((half, 16, slim), low), pltpu.SemaphoreType.DMA((half,))],
        0,
        32 * slim * half,
        where, lags, *first, alias=half, far_out=True,
    )
    first = [first[0]] + [swap(first[k], k, count) for k in range(1, half)]
    sums = sum(value[rows:, 0:LANES].astype(jnp.float32) for value in first)
    sums = sums[: 2 * nfil] + sums[2 * nfil :]
    mine, other = sums[:nfil], sums[nfil:]
    scale = (total * (D // NFILT)) ** (-0.5)
    arrived = [across(other, 0, half), across(mine, 2, 0), across(other, 2, half)]
    filter_grad = (mine + sum(arrived)) * scale

    outs = call(
        functools.partial(final_kernel, half, slim),
        [shape((rows, width), low)] * 4,
        [pltpu.VMEM((half, 4, rows, slim), low), pltpu.SemaphoreType.DMA((half, 4))],
        4 * rows * rows * width,
        20 * rows * width,
        where, queries, keys, values, cotangent, *first, *second, far_out=True,
    )
    return (*outs, filter_grad)


def toeplitz(padded, base, height, breadth):
    middle = padded.shape[1] // 2
    span = height + breadth - 1
    window = lax.dynamic_slice_in_dim(padded, middle + base - breadth + 1, span, 1)
    flipped = window[:, ::-1]
    tiled = jnp.tile(flipped, (1, height + 1))
    flat = tiled[:, height - 1 : height - 1 + height * (span - 1)]
    return flat.reshape(padded.shape[0], height, span - 1)[:, :, :breadth]


def diagonal_sums(product):
    nfil, height, breadth = product.shape
    stride = height + breadth
    flipped = product[:, :, ::-1]
    padded = jnp.pad(flipped, ((0, 0), (0, 0), (0, height)))
    flat = padded.reshape(nfil, height * stride)[:, : height * (stride - 1)]
    return jnp.sum(flat.reshape(nfil, height, stride - 1), axis=1)


def add_lags(lag_acc, sums, first_lag):
    middle = lag_acc.shape[1] // 2
    where = middle + first_lag
    current = lax.dynamic_slice_in_dim(lag_acc, where, sums.shape[1], 1)
    return lax.dynamic_update_slice_in_dim(lag_acc, current + sums, where, 1)


def channel_plan(queries, keys, values, filters, cotangent):
    rows, width = queries.shape
    nfil = filters.shape[0]
    gated = (keys.astype(jnp.float32) * values.astype(jnp.float32)).astype(jnp.bfloat16)
    back = (cotangent.astype(jnp.float32) * queries.astype(jnp.float32)).astype(jnp.bfloat16)
    taps = lax.all_gather(filters, "ctx", axis=1, tiled=True)
    total = taps.shape[1]
    padded = jnp.concatenate([jnp.zeros_like(taps), taps], axis=1)
    lag_start = jnp.zeros((nfil, 2 * total), jnp.float32)
    chan_gated, chan_back = (
        lax.all_to_all(gated, "ctx", split_axis=1, concat_axis=0, tiled=True),
        lax.all_to_all(back, "ctx", split_axis=1, concat_axis=0, tiled=True),
    )
    blocks = total // rows
    slim = chan_gated.shape[1] // nfil
    gated_cols = chan_gated.reshape(blocks, rows, slim, nfil)
    back_cols = chan_back.reshape(blocks, rows, slim, nfil)
    gated_pad = jnp.concatenate([jnp.zeros_like(gated_cols), gated_cols], axis=0)
    back_pad = jnp.concatenate([back_cols, jnp.zeros_like(back_cols)], axis=0)

    def turn(offset, carry):
        mixed_acc, grad_acc, lag_acc = carry
        tile = toeplitz(padded, offset * rows, rows, rows)
        earlier = lax.dynamic_slice_in_dim(gated_pad, blocks - offset, blocks, 0)
        later = lax.dynamic_slice_in_dim(back_pad, offset, blocks, 0)
        mixed_acc = mixed_acc + jnp.einsum(
            "fst,ntcf->nscf", tile, earlier, preferred_element_type=jnp.float32
        )
        grad_acc = grad_acc + jnp.einsum(
            "fst,nscf->ntcf", tile, later, preferred_element_type=jnp.float32
        )
        product = jnp.einsum(
            "nscf,ntcf->fst", back_cols, earlier, preferred_element_type=jnp.float32
        )
        lag_acc = add_lags(lag_acc, diagonal_sums(product), offset * rows - rows + 1)
        return (mixed_acc, grad_acc, lag_acc)

    blank = jnp.zeros((blocks, rows, slim, nfil), jnp.float32)
    mixed_acc, grad_acc, lag_part = lax.fori_loop(0, blocks, turn, (blank, blank, lag_start))
    mixed_chan = mixed_acc.reshape(total, slim * nfil)
    grad_chan = grad_acc.reshape(total, slim * nfil)
    mixed, gated_grad = (
        lax.all_to_all(mixed_chan, "ctx", split_axis=0, concat_axis=1, tiled=True),
        lax.all_to_all(grad_chan, "ctx", split_axis=0, concat_axis=1, tiled=True),
    )
    lag_share = lax.psum_scatter(
        lag_part[:, total:].astype(jnp.bfloat16), "ctx", scatter_dimension=1, tiled=True
    ).astype(jnp.float32)
    lag_total = lax.psum(lag_share, "chan")
    scale = (total * (D // NFILT)) ** (-0.5)
    filter_grad = lag_total * scale
    output = (queries.astype(jnp.float32) * mixed).astype(jnp.bfloat16)
    query_grad = (cotangent.astype(jnp.float32) * mixed).astype(jnp.bfloat16)
    key_grad = (gated_grad * values.astype(jnp.float32)).astype(jnp.bfloat16)
    value_grad = (gated_grad * keys.astype(jnp.float32)).astype(jnp.bfloat16)
    return (output, query_grad, key_grad, value_grad, filter_grad)


def solution(mesh):
    count, chans = mesh.shape["ctx"], mesh.shape["chan"]

    def shards(queries, keys, values, filters, cotangent):
        width = queries.shape[1]
        quarter = width // max(count // 2, 1)
        if count == 8 and chans == 4 and quarter % (2 * LANES) == 0 and queries.shape[0] == LANES:
            return halves_plan(count, chans, queries, keys, values, filters, cotangent)
        return channel_plan(queries, keys, values, filters, cotangent)

    wide = P("ctx", "chan")
    return jax.shard_map(
        shards,
        mesh=mesh,
        in_specs=(wide, wide, wide, P(None, "ctx"), wide),
        out_specs=(wide, wide, wide, wide, P(None, "ctx")),
        check_vma=False,
    )
```

```python
import functools

import jax
import jax.numpy as jnp
from jax import lax
from jax.experimental import pallas as pl
from jax.experimental.pallas import tpu as pltpu
from jax.sharding import PartitionSpec as P

D = 8192
NFILT = 4
LANES = 128
GRANT = 24 * 2**20


def exchange(size, reverse, dtype):
    row = lax.broadcasted_iota(jnp.int32, (size, size), 0)
    col = lax.broadcasted_iota(jnp.int32, (size, size), 1)
    target = jnp.where(reverse, size - 1 - row, row)
    return jnp.where(col == target, 1.0, 0.0).astype(jnp.float32).astype(dtype)


def exact_rows(matrix, values):
    return jnp.dot(matrix, values, preferred_element_type=jnp.float32).astype(jnp.bfloat16)


def gate_kernel(half, slim, me_ref, q_ref, k_ref, v_ref, g_ref, *refs):
    outs, (pair_ref, held, sems) = refs[:-3], refs[-3:]
    rows = q_ref.shape[0]
    me = me_ref[0]
    upper = me >= half
    copies = []
    for chunk in range(half // 2):
        base = (((me & (half - 1)) // 2) ^ chunk) * 2 * slim
        lanes = pl.ds(pl.multiple_of(base, LANES), 2 * slim)
        copies.append([])
        for index, ref in enumerate((q_ref, k_ref, v_ref, g_ref)):
            copy = pltpu.make_async_copy(
                ref.at[:, lanes], held.at[chunk, index], sems.at[chunk, index]
            )
            copy.start()
            copies[chunk].append(copy)
    turn_other = exchange(rows, jnp.logical_not(upper), jnp.bfloat16)
    for step in range(half):
        if step % 2 == 0:
            for copy in copies[step // 2]:
                copy.wait()
        lanes = pl.ds(pl.multiple_of(((me ^ step) & 1) * slim, LANES), slim)
        q, k, v, g = [held[step // 2, index, :, lanes].astype(jnp.float32) for index in range(4)]
        gated = (k * v).astype(jnp.bfloat16)
        back = (g * q).astype(jnp.bfloat16)
        second = jnp.where(upper, back, gated)
        pair_ref[step, 0] = jnp.where(upper, gated, back)
        pair_ref[step, 1] = second
        outs[step][...] = exact_rows(turn_other, second)


def bundle_kernel(half, me_ref, mine_ref, other_ref, pair_ref, *outs):
    rows = pair_ref.shape[2]
    turn = exchange(rows, me_ref[0] >= half, jnp.bfloat16)
    mine, other = mine_ref[...].astype(jnp.float32), other_ref[...].astype(jnp.float32)
    gap = jnp.zeros((8 - mine.shape[0], LANES), jnp.float32)
    both = jnp.concatenate([mine, gap, other, gap], axis=0).astype(jnp.bfloat16)
    for step in range(half):
        outs[step][0:rows, :] = exact_rows(turn, pair_ref[step, 0])
        outs[step][rows : 2 * rows, :] = exact_rows(turn, pair_ref[step, 1])
        outs[step][2 * rows :, :] = jnp.zeros((16, outs[step].shape[1]), jnp.bfloat16)
        outs[step][2 * rows :, 0:LANES] = both


def fill_bands(half, me, arrived, near_ref, far_ref, line):
    nfil, size, total = near_ref.shape
    for step in range(half):
        both = arrived[step][arrived[step].shape[0] - 16 :, 0:LANES].astype(jnp.float32)
        for index, source in enumerate((me ^ step, me ^ step ^ half)):
            place = pl.multiple_of(source * LANES, LANES)
            line[:, pl.ds(place, LANES)] = both[8 * index : 8 * index + 8, :]
    row = lax.broadcasted_iota(jnp.int32, (size, total), 0)
    col = lax.broadcasted_iota(jnp.int32, (size, total), 1)
    reach = far_ref.shape[2] // size
    for index in range(nfil):
        spread = jnp.broadcast_to(line[index : index + 1, :], (size, total))
        rolled = pltpu.roll(spread, 0, 1, stride=1, stride_axis=0)
        band = jnp.where(col >= row, rolled, 0.0)
        near_ref[index] = band.astype(jnp.bfloat16)
        for block in range(reach):
            piece = band[:, (reach - 1 - block) * size : (reach - block) * size]
            far_ref[index, :, block * size : (block + 1) * size] = piece.T.astype(jnp.bfloat16)


def slot_of(half, me, step):
    return ((me ^ step) & (half - 1)) ^ jnp.where(me >= half, half - 1, 0)


def rows_at(slot, rows):
    return pl.ds(pl.multiple_of(slot * rows, rows), rows)


def products(left, right):
    contract = (((1,), (1,)), ((), ()))
    return lax.dot_general(left, right, contract, preferred_element_type=jnp.float32)


def add_columns(columns, values, start):
    first = start // LANES
    for index in range(values.shape[1] // LANES):
        piece = values[:, index * LANES : (index + 1) * LANES]
        have = columns[first + index]
        columns[first + index] = piece if have is None else have + piece


def joined_columns(columns, rows):
    blank = jnp.zeros((rows, LANES), jnp.float32)
    return jnp.concatenate([blank if c is None else c for c in columns], axis=1)


def diagonal_rows(acc):
    rolled = pltpu.roll(acc, 0, 1, stride=1, stride_axis=0)
    return jnp.broadcast_to(jnp.sum(rolled, axis=0, keepdims=True), (8, acc.shape[1]))


def pair_base(half, me, pair, rows):
    slot = slot_of(half, me, 2 * pair)
    return pl.multiple_of((slot // 2) * 2 * rows, 2 * rows)


def stack_pair(half, me, pair, arrived, target, rows):
    for index in range(2):
        place = (slot_of(half, me, 2 * pair + index) % 2) * rows
        target[pl.ds(pl.multiple_of(place, rows), rows), :] = arrived[index][...]


def outer_lags(half, me, base, pair_ref, flip_ref, lag_ref):
    own, width = flip_ref.shape
    rows = own // half
    reach = pair_ref.shape[0]
    share = width // 2
    window = own + reach
    lanes = pl.ds(pl.multiple_of(jnp.where(me >= half, share, 0), LANES), share)
    for index in range(NFILT):
        right = pair_ref[:, lanes] * lane_mask(share, NFILT, index)
        columns = [None] * (window // LANES)
        every = products(flip_ref[:, lanes], right)
        for start in range(0, own, rows):
            add_columns(columns, every[start : start + rows, :], own - rows - start)
        sums = pltpu.roll(diagonal_rows(joined_columns(columns, rows)), 1, 1)
        lag_ref[index : index + 1, pl.ds(base, window)] += sums[0:1, :]


def outer_rows(half, top, base, near_ref, pair_ref):
    nfil, size, total = near_ref.shape
    reach, width = pair_ref.shape
    acc = jnp.zeros((size, width), jnp.float32)
    for index in range(nfil):
        start = pl.multiple_of(total // 2 - top + base, reach)
        acc += jnp.dot(
            near_ref[index, :, pl.ds(start, reach)],
            pair_ref[...] * lane_mask(width, nfil, index),
            preferred_element_type=jnp.float32,
        )
    return acc


def lane_mask(width, nfil, index):
    lane = lax.broadcasted_iota(jnp.int32, (1, width), 1)
    return jnp.where(lane % nfil == index, 1.0, 0.0).astype(jnp.bfloat16)


def inner_kernel(half, me_ref, *refs):
    arrived, across = refs[:half], refs[half : half + 2]
    outs = refs[half + 2 : 2 * half + 2]
    near_ref, part_ref, flip_ref, lag_ref = refs[2 * half + 2 : 2 * half + 6]
    far_ref, line, first_ref, second_ref, pair_ref, result_ref = refs[2 * half + 6 :]
    nfil, size, total = near_ref.shape
    own, width = second_ref.shape
    rows = own // half
    me = me_ref[0]
    turn = exchange(rows, True, jnp.bfloat16)
    fill_bands(half, me, arrived, near_ref, far_ref, line)
    for step in range(half):
        where = rows_at(slot_of(half, me, step), rows)
        first_ref[where, :] = arrived[step][0:rows, :]
        second_ref[where, :] = arrived[step][rows : 2 * rows, :]
        flip_ref[where, :] = exact_rows(turn, arrived[step][rows : 2 * rows, :])
    stack_pair(half, me, 0, across, pair_ref, rows)
    base = pair_base(half, me, 0, rows)
    masks = [lane_mask(width, nfil, index) for index in range(nfil)]
    for top in range(0, own, size):
        acc = jnp.zeros((size, width), jnp.float32)
        for index in range(nfil):
            acc += jnp.dot(
                far_ref[index, :, own - size - top : own],
                second_ref[0 : top + size, :] * masks[index],
                preferred_element_type=jnp.float32,
            )
        result_ref[top : top + size, :] = acc.astype(jnp.bfloat16)
    for step in range(half):
        outs[step][...] = result_ref[rows_at(slot_of(half, me, step), rows), :]
    for top in range(0, own, size):
        acc = outer_rows(half, top, base, near_ref, pair_ref)
        for index in range(nfil):
            acc += jnp.dot(
                near_ref[index, :, 0 : own - top],
                first_ref[top:own, :] * masks[index],
                preferred_element_type=jnp.float32,
            )
        part_ref[top : top + size, :] = acc
    lag_ref[...] = jnp.zeros((8, total), jnp.float32)
    for index in range(nfil):
        columns = [None] * ((own + rows) // LANES)
        every = products(flip_ref[...], first_ref[...] * masks[index])
        for start in range(0, own, rows):
            add_columns(columns, every[start : start + rows, start:own], 0)
        sums = pltpu.roll(diagonal_rows(joined_columns(columns, rows)), own + 1, 1)
        lag_ref[index : index + 1, 0:own] = sums[0:1, 0:own]
    outer_lags(half, me, base, pair_ref, flip_ref, lag_ref)


def lag_kernel(half, me_ref, *refs):
    across = refs[:2]
    flip_ref, lag_ref, out_ref, pair_ref = refs[2:]
    rows = flip_ref.shape[0] // half
    me = me_ref[0]
    stack_pair(half, me, 1, across, pair_ref, rows)
    out_ref[...] = lag_ref[...]
    outer_lags(half, me, pair_base(half, me, 1, rows), pair_ref, flip_ref, out_ref)


def attach_kernel(half, me_ref, lag_ref, *refs):
    outs, (held, sems) = refs[half : 2 * half], refs[2 * half :]
    rows = outs[0].shape[0] - 16
    nfil = NFILT
    me = me_ref[0]
    copies = []
    for step in range(half):
        pieces = []
        for target in (me ^ step, me ^ step ^ half):
            place = pl.multiple_of(target * LANES, LANES)
            pieces.append(lag_ref[0:nfil, pl.ds(place, LANES)])
        both = jnp.concatenate(pieces, axis=0)
        high = both.astype(jnp.bfloat16).astype(jnp.float32)
        rest = (both - high).astype(jnp.bfloat16).astype(jnp.float32)
        held[step] = jnp.zeros(held.shape[1:], jnp.bfloat16)
        held[step, :, 0:LANES] = jnp.concatenate([high, rest], axis=0).astype(jnp.bfloat16)
        copy = pltpu.make_async_copy(held.at[step], outs[step].at[rows : rows + 16], sems.at[step])
        copy.start()
        copies.append(copy)
    for copy in copies:
        copy.wait()


def outer_kernel(half, me_ref, *refs):
    across = refs[:2]
    near_ref, part_ref = refs[2:4]
    outs = refs[4 : half + 4]
    pair_ref, result_ref = refs[half + 4 :]
    nfil, size, total = near_ref.shape
    own, width = part_ref.shape
    rows = own // half
    me = me_ref[0]
    stack_pair(half, me, 1, across, pair_ref, rows)
    base = pair_base(half, me, 1, rows)
    for top in range(0, own, size):
        acc = part_ref[top : top + size, :] + outer_rows(half, top, base, near_ref, pair_ref)
        result_ref[top : top + size, :] = acc.astype(jnp.bfloat16)
    for step in range(half):
        outs[step][0:rows, :] = result_ref[rows_at(slot_of(half, me, step), rows), :]


def final_kernel(half, slim, me_ref, q_ref, k_ref, v_ref, g_ref, *refs):
    firsts = [refs[0], *refs[half - 1 : 0 : -1]]
    seconds = [refs[half], *refs[2 * half - 1 : half : -1]]
    outs = refs[2 * half : 2 * half + 4]
    held, sems = refs[2 * half + 4 :]
    rows = q_ref.shape[0]
    me = me_ref[0]
    upper = me >= half
    turn = exchange(rows, upper, jnp.bfloat16)
    copies = []
    for step in range(half):
        part = (me ^ step) & (half - 1)
        lanes = pl.ds(pl.multiple_of(part * slim, LANES), slim)
        first = jnp.dot(turn, firsts[step][0:rows, :], preferred_element_type=jnp.float32)
        second = jnp.dot(turn, seconds[step][...], preferred_element_type=jnp.float32)
        mixed = jnp.where(upper, first, second)
        grad = jnp.where(upper, second, first)
        for index, (ref, value) in enumerate(
            ((q_ref, mixed), (g_ref, mixed), (v_ref, grad), (k_ref, grad))
        ):
            held[step, index] = (ref[:, lanes].astype(jnp.float32) * value).astype(jnp.bfloat16)
            copy = pltpu.make_async_copy(
                held.at[step, index], outs[index].at[:, lanes], sems.at[step, index]
            )
            copy.start()
            copies.append(copy)
    for copy in copies:
        copy.wait()


def swap(value, step, count):
    return lax.ppermute(value, "ctx", [(i, i ^ step) for i in range(count)])


def after(value, *earlier):
    return lax.optimization_barrier((value, *earlier))


def call(kernel, outs, scratch, flops, nbytes, *args, far=0, far_out=False, alias=0):
    near_spec, far_spec = pl.BlockSpec(memory_space=pltpu.VMEM), pl.BlockSpec(memory_space=pl.ANY)
    near = len(args) - 1 - far - alias
    return pl.pallas_call(
        kernel,
        out_shape=outs,
        in_specs=[pl.BlockSpec(memory_space=pltpu.SMEM)]
        + [far_spec] * far
        + [near_spec] * near
        + [far_spec] * alias,
        out_specs=[far_spec if far_out else near_spec] * len(outs),
        scratch_shapes=scratch,
        input_output_aliases={len(args) - alias + k: k for k in range(alias)},
        compiler_params=pltpu.CompilerParams(vmem_limit_bytes=GRANT),
        cost_estimate=pl.CostEstimate(flops=flops, bytes_accessed=nbytes, transcendentals=0),
    )(*args)


def halves_plan(count, chans, queries, keys, values, filters, cotangent):
    rows, width = queries.shape
    nfil = filters.shape[0]
    half = count // 2
    slim = width // half
    total = count * rows
    own = half * rows
    size = min(256, own)
    low = jnp.bfloat16
    shape = jax.ShapeDtypeStruct
    me = lax.axis_index("ctx")
    where = me.astype(jnp.int32).reshape(1)

    other_taps = swap(filters, half, count)
    branches = [
        pltpu.with_memory_space_constraint(x, pltpu.HBM)
        for x in (queries, keys, values, cotangent)
    ]
    *sent, pair = call(
        functools.partial(gate_kernel, half, slim),
        [shape((rows, slim), low)] * half + [shape((half, 2, rows, slim), low)],
        [pltpu.VMEM((half // 2, 4, rows, 2 * slim), low), pltpu.SemaphoreType.DMA((half // 2, 4))],
        2 * rows * rows * width,
        14 * rows * width,
        where, *branches, far=4,
    )
    inner = call(
        functools.partial(bundle_kernel, half),
        [shape((2 * rows + 16, slim), low)] * half,
        [],
        4 * rows * rows * width,
        8 * rows * width,
        where, filters, other_taps, pair,
    )
    inner = [inner[0]] + [swap(inner[k], k, count) for k in range(1, half)]
    outer = list(sent)
    outer[0] = swap(outer[0], half, count)
    outer[1] = swap(outer[1], half + 1, count)
    outer[2], inner[1] = after(outer[2], inner[1])
    outer[2] = swap(outer[2], half + 2, count)
    outer[3], inner[2] = after(outer[3], inner[2])
    outer[3] = swap(outer[3], half + 3, count)

    *second, near, part, flipped, lags = call(
        functools.partial(inner_kernel, half),
        [shape((rows, slim), low)] * half
        + [
            shape((nfil, size, total), low),
            shape((own, slim), jnp.float32),
            shape((own, slim), low),
            shape((8, total), jnp.float32),
        ],
        [
            pltpu.VMEM((nfil, size, own), low),
            pltpu.VMEM((8, total), jnp.float32),
            pltpu.VMEM((own, slim), low),
            pltpu.VMEM((own, slim), low),
            pltpu.VMEM((2 * rows, slim), low),
            pltpu.VMEM((own, slim), low),
        ],
        8 * nfil * own * slim * own,
        8 * own * slim,
        where, *inner, *outer[:2],
    )
    second = [second[0]] + [swap(second[k], k, count) for k in range(half - 1, 0, -1)][::-1]
    across = lambda value, move, turn: lax.ppermute(
        value,
        ("chan", "ctx"),
        [(c * count + i, (c ^ move) * count + (i ^ turn)) for c in range(chans) for i in range(count)],
    )
    (lags,) = call(
        functools.partial(lag_kernel, half),
        [shape((8, total), jnp.float32)],
        [pltpu.VMEM((2 * rows, slim), low)],
        nfil * own * slim * own // 2,
        own * slim,
        where, *outer[2:], flipped, lags,
    )
    outer[2], lags = after(outer[2], lags)
    first = call(
        functools.partial(outer_kernel, half),
        [shape((rows + 16, slim), low)] * half,
        [pltpu.VMEM((2 * rows, slim), low), pltpu.VMEM((own, slim), low)],
        nfil * own * slim * own,
        4 * own * slim,
        where, *outer[2:], near, part,
    )
    lags = lags + across(lags, 1, 0)
    first = call(
        functools.partial(attach_kernel, half),
        [shape((rows + 16, slim), low)] * half,
        [pltpu.VMEM((half, 16, slim), low), pltpu.SemaphoreType.DMA((half,))],
        0,
        32 * slim * half,
        where, lags, *first, alias=half, far_out=True,
    )
    first = [first[0]] + [swap(first[k], k, count) for k in range(half - 1, 0, -1)][::-1]
    sums = sum(value[rows:, 0:LANES].astype(jnp.float32) for value in first)
    sums = sums[: 2 * nfil] + sums[2 * nfil :]
    mine, other = sums[:nfil], sums[nfil:]
    scale = (total * (D // NFILT)) ** (-0.5)
    arrived = [across(other, 0, half), across(mine, 2, 0), across(other, 2, half)]
    filter_grad = (mine + sum(arrived)) * scale

    outs = call(
        functools.partial(final_kernel, half, slim),
        [shape((rows, width), low)] * 4,
        [pltpu.VMEM((half, 4, rows, slim), low), pltpu.SemaphoreType.DMA((half, 4))],
        4 * rows * rows * width,
        20 * rows * width,
        where, queries, keys, values, cotangent, first[0], *first[:0:-1], second[0], *second[:0:-1], far_out=True,
    )
    return (*outs, filter_grad)


def toeplitz(padded, base, height, breadth):
    middle = padded.shape[1] // 2
    span = height + breadth - 1
    window = lax.dynamic_slice_in_dim(padded, middle + base - breadth + 1, span, 1)
    flipped = window[:, ::-1]
    tiled = jnp.tile(flipped, (1, height + 1))
    flat = tiled[:, height - 1 : height - 1 + height * (span - 1)]
    return flat.reshape(padded.shape[0], height, span - 1)[:, :, :breadth]


def diagonal_sums(product):
    nfil, height, breadth = product.shape
    stride = height + breadth
    flipped = product[:, :, ::-1]
    padded = jnp.pad(flipped, ((0, 0), (0, 0), (0, height)))
    flat = padded.reshape(nfil, height * stride)[:, : height * (stride - 1)]
    return jnp.sum(flat.reshape(nfil, height, stride - 1), axis=1)


def add_lags(lag_acc, sums, first_lag):
    middle = lag_acc.shape[1] // 2
    where = middle + first_lag
    current = lax.dynamic_slice_in_dim(lag_acc, where, sums.shape[1], 1)
    return lax.dynamic_update_slice_in_dim(lag_acc, current + sums, where, 1)


def channel_plan(queries, keys, values, filters, cotangent):
    rows, width = queries.shape
    nfil = filters.shape[0]
    gated = (keys.astype(jnp.float32) * values.astype(jnp.float32)).astype(jnp.bfloat16)
    back = (cotangent.astype(jnp.float32) * queries.astype(jnp.float32)).astype(jnp.bfloat16)
    taps = lax.all_gather(filters, "ctx", axis=1, tiled=True)
    total = taps.shape[1]
    padded = jnp.concatenate([jnp.zeros_like(taps), taps], axis=1)
    lag_start = jnp.zeros((nfil, 2 * total), jnp.float32)
    chan_gated, chan_back = (
        lax.all_to_all(gated, "ctx", split_axis=1, concat_axis=0, tiled=True),
        lax.all_to_all(back, "ctx", split_axis=1, concat_axis=0, tiled=True),
    )
    blocks = total // rows
    slim = chan_gated.shape[1] // nfil
    gated_cols = chan_gated.reshape(blocks, rows, slim, nfil)
    back_cols = chan_back.reshape(blocks, rows, slim, nfil)
    gated_pad = jnp.concatenate([jnp.zeros_like(gated_cols), gated_cols], axis=0)
    back_pad = jnp.concatenate([back_cols, jnp.zeros_like(back_cols)], axis=0)

    def turn(offset, carry):
        mixed_acc, grad_acc, lag_acc = carry
        tile = toeplitz(padded, offset * rows, rows, rows)
        earlier = lax.dynamic_slice_in_dim(gated_pad, blocks - offset, blocks, 0)
        later = lax.dynamic_slice_in_dim(back_pad, offset, blocks, 0)
        mixed_acc = mixed_acc + jnp.einsum(
            "fst,ntcf->nscf", tile, earlier, preferred_element_type=jnp.float32
        )
        grad_acc = grad_acc + jnp.einsum(
            "fst,nscf->ntcf", tile, later, preferred_element_type=jnp.float32
        )
        product = jnp.einsum(
            "nscf,ntcf->fst", back_cols, earlier, preferred_element_type=jnp.float32
        )
        lag_acc = add_lags(lag_acc, diagonal_sums(product), offset * rows - rows + 1)
        return (mixed_acc, grad_acc, lag_acc)

    blank = jnp.zeros((blocks, rows, slim, nfil), jnp.float32)
    mixed_acc, grad_acc, lag_part = lax.fori_loop(0, blocks, turn, (blank, blank, lag_start))
    mixed_chan = mixed_acc.reshape(total, slim * nfil)
    grad_chan = grad_acc.reshape(total, slim * nfil)
    mixed, gated_grad = (
        lax.all_to_all(mixed_chan, "ctx", split_axis=0, concat_axis=1, tiled=True),
        lax.all_to_all(grad_chan, "ctx", split_axis=0, concat_axis=1, tiled=True),
    )
    lag_share = lax.psum_scatter(
        lag_part[:, total:].astype(jnp.bfloat16), "ctx", scatter_dimension=1, tiled=True
    ).astype(jnp.float32)
    lag_total = lax.psum(lag_share, "chan")
    scale = (total * (D // NFILT)) ** (-0.5)
    filter_grad = lag_total * scale
    output = (queries.astype(jnp.float32) * mixed).astype(jnp.bfloat16)
    query_grad = (cotangent.astype(jnp.float32) * mixed).astype(jnp.bfloat16)
    key_grad = (gated_grad * values.astype(jnp.float32)).astype(jnp.bfloat16)
    value_grad = (gated_grad * keys.astype(jnp.float32)).astype(jnp.bfloat16)
    return (output, query_grad, key_grad, value_grad, filter_grad)


def solution(mesh):
    count, chans = mesh.shape["ctx"], mesh.shape["chan"]

    def shards(queries, keys, values, filters, cotangent):
        width = queries.shape[1]
        quarter = width // max(count // 2, 1)
        if count == 8 and chans == 4 and quarter % (2 * LANES) == 0 and queries.shape[0] == LANES:
            return halves_plan(count, chans, queries, keys, values, filters, cotangent)
        return channel_plan(queries, keys, values, filters, cotangent)

    wide = P("ctx", "chan")
    return jax.shard_map(
        shards,
        mesh=mesh,
        in_specs=(wide, wide, wide, P(None, "ctx"), wide),
        out_specs=(wide, wide, wide, wide, P(None, "ctx")),
        check_vma=False,
    )
```

```python
import functools

import jax
import jax.numpy as jnp
from jax import lax
from jax.experimental import pallas as pl
from jax.experimental.pallas import tpu as pltpu
from jax.sharding import PartitionSpec as P

D = 8192
NFILT = 4
LANES = 128
GRANT = 24 * 2**20


def exchange(size, reverse, dtype):
    row = lax.broadcasted_iota(jnp.int32, (size, size), 0)
    col = lax.broadcasted_iota(jnp.int32, (size, size), 1)
    target = jnp.where(reverse, size - 1 - row, row)
    return jnp.where(col == target, 1.0, 0.0).astype(jnp.float32).astype(dtype)


def exact_rows(matrix, values):
    return jnp.dot(matrix, values, preferred_element_type=jnp.float32).astype(jnp.bfloat16)


def gate_kernel(half, slim, me_ref, q_ref, k_ref, v_ref, g_ref, *refs):
    outs, (held, sems) = refs[:-2], refs[-2:]
    rows = q_ref.shape[0]
    me = me_ref[0]
    upper = me >= half
    copies = []
    for chunk in range(half // 2):
        base = (((me & (half - 1)) // 2) ^ chunk) * 2 * slim
        lanes = pl.ds(pl.multiple_of(base, LANES), 2 * slim)
        copies.append([])
        for index, ref in enumerate((q_ref, k_ref, v_ref, g_ref)):
            copy = pltpu.make_async_copy(
                ref.at[:, lanes], held.at[chunk, index], sems.at[chunk, index]
            )
            copy.start()
            copies[chunk].append(copy)
    turn = exchange(rows, upper, jnp.bfloat16)
    turn_other = exchange(rows, jnp.logical_not(upper), jnp.bfloat16)
    for step in range(half):
        if step % 2 == 0:
            for copy in copies[step // 2]:
                copy.wait()
        lanes = pl.ds(pl.multiple_of(((me ^ step) & 1) * slim, LANES), slim)
        q, k, v, g = [held[step // 2, index, :, lanes].astype(jnp.float32) for index in range(4)]
        gated = (k * v).astype(jnp.bfloat16)
        back = (g * q).astype(jnp.bfloat16)
        second = jnp.where(upper, back, gated)
        outs[step][...] = exact_rows(turn_other, second)
        bundle = outs[half + step]
        bundle[0:rows, :] = exact_rows(turn, jnp.where(upper, gated, back))
        bundle[rows : 2 * rows, :] = exact_rows(turn, second)


def label_kernel(half, me_ref, mine_ref, other_ref, *refs):
    outs, (held, sems) = refs[half : 2 * half], refs[2 * half :]
    rows = outs[0].shape[0] - 16
    mine, other = mine_ref[...].astype(jnp.float32), other_ref[...].astype(jnp.float32)
    gap = jnp.zeros((8 - mine.shape[0], LANES), jnp.float32)
    held[...] = jnp.zeros(held.shape, jnp.bfloat16)
    held[:, 0:LANES] = jnp.concatenate([mine, gap, other, gap], axis=0).astype(jnp.bfloat16)
    copies = [
        pltpu.make_async_copy(held, outs[step].at[rows : rows + 16], sems.at[step])
        for step in range(half)
    ]
    for copy in copies:
        copy.start()
    for copy in copies:
        copy.wait()


def fill_bands(half, me, arrived, near_ref, far_ref, line):
    nfil, size, total = near_ref.shape
    for step in range(half):
        both = arrived[step][arrived[step].shape[0] - 16 :, 0:LANES].astype(jnp.float32)
        for index, source in enumerate((me ^ step, me ^ step ^ half)):
            place = pl.multiple_of(source * LANES, LANES)
            line[:, pl.ds(place, LANES)] = both[8 * index : 8 * index + 8, :]
    row = lax.broadcasted_iota(jnp.int32, (size, total), 0)
    col = lax.broadcasted_iota(jnp.int32, (size, total), 1)
    reach = far_ref.shape[2] // size
    for index in range(nfil):
        spread = jnp.broadcast_to(line[index : index + 1, :], (size, total))
        rolled = pltpu.roll(spread, 0, 1, stride=1, stride_axis=0)
        band = jnp.where(col >= row, rolled, 0.0)
        near_ref[index] = band.astype(jnp.bfloat16)
        for block in range(reach):
            piece = band[:, (reach - 1 - block) * size : (reach - block) * size]
            far_ref[index, :, block * size : (block + 1) * size] = piece.T.astype(jnp.bfloat16)


def slot_of(half, me, step):
    return ((me ^ step) & (half - 1)) ^ jnp.where(me >= half, half - 1, 0)


def rows_at(slot, rows):
    return pl.ds(pl.multiple_of(slot * rows, rows), rows)


def products(left, right):
    contract = (((1,), (1,)), ((), ()))
    return lax.dot_general(left, right, contract, preferred_element_type=jnp.float32)


def add_columns(columns, values, start):
    first = start // LANES
    for index in range(values.shape[1] // LANES):
        piece = values[:, index * LANES : (index + 1) * LANES]
        have = columns[first + index]
        columns[first + index] = piece if have is None else have + piece


def joined_columns(columns, rows):
    blank = jnp.zeros((rows, LANES), jnp.float32)
    return jnp.concatenate([blank if c is None else c for c in columns], axis=1)


def diagonal_rows(acc):
    rolled = pltpu.roll(acc, 0, 1, stride=1, stride_axis=0)
    return jnp.broadcast_to(jnp.sum(rolled, axis=0, keepdims=True), (8, acc.shape[1]))


def pair_base(half, me, pair, rows):
    slot = slot_of(half, me, 2 * pair)
    return pl.multiple_of((slot // 2) * 2 * rows, 2 * rows)


def stack_pair(half, me, pair, arrived, target, rows):
    for index in range(2):
        place = (slot_of(half, me, 2 * pair + index) % 2) * rows
        target[pl.ds(pl.multiple_of(place, rows), rows), :] = arrived[index][...]


def outer_lags(half, me, base, pair_ref, flip_ref, lag_ref):
    own, width = flip_ref.shape
    rows = own // half
    reach = pair_ref.shape[0]
    share = width // 2
    window = own + reach
    lanes = pl.ds(pl.multiple_of(jnp.where(me >= half, share, 0), LANES), share)
    for index in range(NFILT):
        right = pair_ref[:, lanes] * lane_mask(share, NFILT, index)
        columns = [None] * (window // LANES)
        every = products(flip_ref[:, lanes], right)
        for start in range(0, own, rows):
            add_columns(columns, every[start : start + rows, :], own - rows - start)
        sums = pltpu.roll(diagonal_rows(joined_columns(columns, rows)), 1, 1)
        lag_ref[index : index + 1, pl.ds(base, window)] += sums[0:1, :]


def outer_rows(half, top, base, near_ref, pair_ref):
    nfil, size, total = near_ref.shape
    reach, width = pair_ref.shape
    acc = jnp.zeros((size, width), jnp.float32)
    for index in range(nfil):
        start = pl.multiple_of(total // 2 - top + base, reach)
        acc += jnp.dot(
            near_ref[index, :, pl.ds(start, reach)],
            pair_ref[...] * lane_mask(width, nfil, index),
            preferred_element_type=jnp.float32,
        )
    return acc


def lane_mask(width, nfil, index):
    lane = lax.broadcasted_iota(jnp.int32, (1, width), 1)
    return jnp.where(lane % nfil == index, 1.0, 0.0).astype(jnp.bfloat16)


def inner_kernel(half, me_ref, *refs):
    arrived, across = refs[:half], refs[half : half + 2]
    outs = refs[half + 2 : 2 * half + 2]
    near_ref, part_ref, flip_ref, lag_ref = refs[2 * half + 2 : 2 * half + 6]
    far_ref, line, first_ref, second_ref, pair_ref, result_ref = refs[2 * half + 6 :]
    nfil, size, total = near_ref.shape
    own, width = second_ref.shape
    rows = own // half
    me = me_ref[0]
    turn = exchange(rows, True, jnp.bfloat16)
    fill_bands(half, me, arrived, near_ref, far_ref, line)
    for step in range(half):
        where = rows_at(slot_of(half, me, step), rows)
        first_ref[where, :] = arrived[step][0:rows, :]
        second_ref[where, :] = arrived[step][rows : 2 * rows, :]
        flip_ref[where, :] = exact_rows(turn, arrived[step][rows : 2 * rows, :])
    stack_pair(half, me, 0, across, pair_ref, rows)
    base = pair_base(half, me, 0, rows)
    masks = [lane_mask(width, nfil, index) for index in range(nfil)]
    for top in range(0, own, size):
        acc = jnp.zeros((size, width), jnp.float32)
        for index in range(nfil):
            acc += jnp.dot(
                far_ref[index, :, own - size - top : own],
                second_ref[0 : top + size, :] * masks[index],
                preferred_element_type=jnp.float32,
            )
        result_ref[top : top + size, :] = acc.astype(jnp.bfloat16)
    for step in range(half):
        outs[step][...] = result_ref[rows_at(slot_of(half, me, step), rows), :]
    for top in range(0, own, size):
        acc = outer_rows(half, top, base, near_ref, pair_ref)
        for index in range(nfil):
            acc += jnp.dot(
                near_ref[index, :, 0 : own - top],
                first_ref[top:own, :] * masks[index],
                preferred_element_type=jnp.float32,
            )
        part_ref[top : top + size, :] = acc
    lag_ref[...] = jnp.zeros((8, total), jnp.float32)
    for index in range(nfil):
        columns = [None] * ((own + rows) // LANES)
        every = products(flip_ref[...], first_ref[...] * masks[index])
        for start in range(0, own, rows):
            add_columns(columns, every[start : start + rows, start:own], 0)
        sums = pltpu.roll(diagonal_rows(joined_columns(columns, rows)), own + 1, 1)
        lag_ref[index : index + 1, 0:own] = sums[0:1, 0:own]
    outer_lags(half, me, base, pair_ref, flip_ref, lag_ref)


def lag_kernel(half, me_ref, *refs):
    across = refs[:2]
    flip_ref, lag_ref, out_ref, pair_ref = refs[2:]
    rows = flip_ref.shape[0] // half
    me = me_ref[0]
    stack_pair(half, me, 1, across, pair_ref, rows)
    out_ref[...] = lag_ref[...]
    outer_lags(half, me, pair_base(half, me, 1, rows), pair_ref, flip_ref, out_ref)


def attach_kernel(half, me_ref, lag_ref, *refs):
    outs, (held, sems) = refs[half : 2 * half], refs[2 * half :]
    rows = outs[0].shape[0] - 16
    nfil = NFILT
    me = me_ref[0]
    copies = []
    for step in range(half):
        pieces = []
        for target in (me ^ step, me ^ step ^ half):
            place = pl.multiple_of(target * LANES, LANES)
            pieces.append(lag_ref[0:nfil, pl.ds(place, LANES)])
        both = jnp.concatenate(pieces, axis=0)
        high = both.astype(jnp.bfloat16).astype(jnp.float32)
        rest = (both - high).astype(jnp.bfloat16).astype(jnp.float32)
        held[step] = jnp.zeros(held.shape[1:], jnp.bfloat16)
        held[step, :, 0:LANES] = jnp.concatenate([high, rest], axis=0).astype(jnp.bfloat16)
        copy = pltpu.make_async_copy(held.at[step], outs[step].at[rows : rows + 16], sems.at[step])
        copy.start()
        copies.append(copy)
    for copy in copies:
        copy.wait()


def outer_kernel(half, me_ref, *refs):
    across = refs[:2]
    near_ref, part_ref = refs[2:4]
    outs = refs[4 : half + 4]
    pair_ref, result_ref = refs[half + 4 :]
    nfil, size, total = near_ref.shape
    own, width = part_ref.shape
    rows = own // half
    me = me_ref[0]
    stack_pair(half, me, 1, across, pair_ref, rows)
    base = pair_base(half, me, 1, rows)
    for top in range(0, own, size):
        acc = part_ref[top : top + size, :] + outer_rows(half, top, base, near_ref, pair_ref)
        result_ref[top : top + size, :] = acc.astype(jnp.bfloat16)
    for step in range(half):
        outs[step][0:rows, :] = result_ref[rows_at(slot_of(half, me, step), rows), :]


def final_kernel(half, slim, me_ref, q_ref, k_ref, v_ref, g_ref, *refs):
    firsts = [refs[0], *refs[half - 1 : 0 : -1]]
    seconds = [refs[half], *refs[2 * half - 1 : half : -1]]
    outs = refs[2 * half : 2 * half + 4]
    held, sems = refs[2 * half + 4 :]
    rows = q_ref.shape[0]
    me = me_ref[0]
    upper = me >= half
    turn = exchange(rows, upper, jnp.bfloat16)
    copies = []
    for step in range(half):
        part = (me ^ step) & (half - 1)
        lanes = pl.ds(pl.multiple_of(part * slim, LANES), slim)
        first = jnp.dot(turn, firsts[step][0:rows, :], preferred_element_type=jnp.float32)
        second = jnp.dot(turn, seconds[step][...], preferred_element_type=jnp.float32)
        mixed = jnp.where(upper, first, second)
        grad = jnp.where(upper, second, first)
        for index, (ref, value) in enumerate(
            ((q_ref, mixed), (g_ref, mixed), (v_ref, grad), (k_ref, grad))
        ):
            held[step, index] = (ref[:, lanes].astype(jnp.float32) * value).astype(jnp.bfloat16)
            copy = pltpu.make_async_copy(
                held.at[step, index], outs[index].at[:, lanes], sems.at[step, index]
            )
            copy.start()
            copies.append(copy)
    for copy in copies:
        copy.wait()


def swap(value, step, count):
    return lax.ppermute(value, "ctx", [(i, i ^ step) for i in range(count)])


def after(value, *earlier):
    return lax.optimization_barrier((value, *earlier))


def call(kernel, outs, scratch, flops, nbytes, *args, far=0, far_out=False, alias=0):
    near_spec, far_spec = pl.BlockSpec(memory_space=pltpu.VMEM), pl.BlockSpec(memory_space=pl.ANY)
    near = len(args) - 1 - far - alias
    return pl.pallas_call(
        kernel,
        out_shape=outs,
        in_specs=[pl.BlockSpec(memory_space=pltpu.SMEM)]
        + [far_spec] * far
        + [near_spec] * near
        + [far_spec] * alias,
        out_specs=[far_spec if far_out else near_spec] * len(outs),
        scratch_shapes=scratch,
        input_output_aliases={len(args) - alias + k: k for k in range(alias)},
        compiler_params=pltpu.CompilerParams(vmem_limit_bytes=GRANT),
        cost_estimate=pl.CostEstimate(flops=flops, bytes_accessed=nbytes, transcendentals=0),
    )(*args)


def halves_plan(count, chans, queries, keys, values, filters, cotangent):
    rows, width = queries.shape
    nfil = filters.shape[0]
    half = count // 2
    slim = width // half
    total = count * rows
    own = half * rows
    size = min(256, own)
    low = jnp.bfloat16
    shape = jax.ShapeDtypeStruct
    me = lax.axis_index("ctx")
    where = me.astype(jnp.int32).reshape(1)

    other_taps = swap(filters, half, count)
    branches = [
        pltpu.with_memory_space_constraint(x, pltpu.HBM)
        for x in (queries, keys, values, cotangent)
    ]
    made = call(
        functools.partial(gate_kernel, half, slim),
        [shape((rows, slim), low)] * half + [shape((2 * rows + 16, slim), low)] * half,
        [pltpu.VMEM((half // 2, 4, rows, 2 * slim), low), pltpu.SemaphoreType.DMA((half // 2, 4))],
        2 * rows * rows * width,
        14 * rows * width,
        where, *branches, far=4,
    )
    sent = made[:half]
    inner = call(
        functools.partial(label_kernel, half),
        [shape((2 * rows + 16, slim), low)] * half,
        [pltpu.VMEM((16, slim), low), pltpu.SemaphoreType.DMA((half,))],
        0,
        64 * slim * half,
        where, filters, other_taps, *made[half:], alias=half, far_out=True,
    )
    inner = [inner[0]] + [swap(inner[k], k, count) for k in range(1, half)]
    outer = list(sent)
    outer[0] = swap(outer[0], half, count)
    outer[1] = swap(outer[1], half + 1, count)
    outer[2], inner[1] = after(outer[2], inner[1])
    outer[2] = swap(outer[2], half + 2, count)
    outer[3], inner[2] = after(outer[3], inner[2])
    outer[3] = swap(outer[3], half + 3, count)

    *second, near, part, flipped, lags = call(
        functools.partial(inner_kernel, half),
        [shape((rows, slim), low)] * half
        + [
            shape((nfil, size, total), low),
            shape((own, slim), jnp.float32),
            shape((own, slim), low),
            shape((8, total), jnp.float32),
        ],
        [
            pltpu.VMEM((nfil, size, own), low),
            pltpu.VMEM((8, total), jnp.float32),
            pltpu.VMEM((own, slim), low),
            pltpu.VMEM((own, slim), low),
            pltpu.VMEM((2 * rows, slim), low),
            pltpu.VMEM((own, slim), low),
        ],
        8 * nfil * own * slim * own,
        8 * own * slim,
        where, *inner, *outer[:2],
    )
    second = [second[0]] + [swap(second[k], k, count) for k in range(half - 1, 0, -1)][::-1]
    across = lambda value, move, turn: lax.ppermute(
        value,
        ("chan", "ctx"),
        [(c * count + i, (c ^ move) * count + (i ^ turn)) for c in range(chans) for i in range(count)],
    )
    (lags,) = call(
        functools.partial(lag_kernel, half),
        [shape((8, total), jnp.float32)],
        [pltpu.VMEM((2 * rows, slim), low)],
        nfil * own * slim * own // 2,
        own * slim,
        where, *outer[2:], flipped, lags,
    )
    outer[2], lags = after(outer[2], lags)
    first = call(
        functools.partial(outer_kernel, half),
        [shape((rows + 16, slim), low)] * half,
        [pltpu.VMEM((2 * rows, slim), low), pltpu.VMEM((own, slim), low)],
        nfil * own * slim * own,
        4 * own * slim,
        where, *outer[2:], near, part,
    )
    lags = lags + across(lags, 1, 0)
    first = call(
        functools.partial(attach_kernel, half),
        [shape((rows + 16, slim), low)] * half,
        [pltpu.VMEM((half, 16, slim), low), pltpu.SemaphoreType.DMA((half,))],
        0,
        32 * slim * half,
        where, lags, *first, alias=half, far_out=True,
    )
    first = [first[0]] + [swap(first[k], k, count) for k in range(half - 1, 0, -1)][::-1]
    sums = sum(value[rows:, 0:LANES].astype(jnp.float32) for value in first)
    sums = sums[: 2 * nfil] + sums[2 * nfil :]
    mine, other = sums[:nfil], sums[nfil:]
    scale = (total * (D // NFILT)) ** (-0.5)
    arrived = [across(other, 0, half), across(mine, 2, 0), across(other, 2, half)]
    filter_grad = (mine + sum(arrived)) * scale

    outs = call(
        functools.partial(final_kernel, half, slim),
        [shape((rows, width), low)] * 4,
        [pltpu.VMEM((half, 4, rows, slim), low), pltpu.SemaphoreType.DMA((half, 4))],
        4 * rows * rows * width,
        20 * rows * width,
        where, queries, keys, values, cotangent, first[0], *first[:0:-1], second[0], *second[:0:-1], far_out=True,
    )
    return (*outs, filter_grad)


def toeplitz(padded, base, height, breadth):
    middle = padded.shape[1] // 2
    span = height + breadth - 1
    window = lax.dynamic_slice_in_dim(padded, middle + base - breadth + 1, span, 1)
    flipped = window[:, ::-1]
    tiled = jnp.tile(flipped, (1, height + 1))
    flat = tiled[:, height - 1 : height - 1 + height * (span - 1)]
    return flat.reshape(padded.shape[0], height, span - 1)[:, :, :breadth]


def diagonal_sums(product):
    nfil, height, breadth = product.shape
    stride = height + breadth
    flipped = product[:, :, ::-1]
    padded = jnp.pad(flipped, ((0, 0), (0, 0), (0, height)))
    flat = padded.reshape(nfil, height * stride)[:, : height * (stride - 1)]
    return jnp.sum(flat.reshape(nfil, height, stride - 1), axis=1)


def add_lags(lag_acc, sums, first_lag):
    middle = lag_acc.shape[1] // 2
    where = middle + first_lag
    current = lax.dynamic_slice_in_dim(lag_acc, where, sums.shape[1], 1)
    return lax.dynamic_update_slice_in_dim(lag_acc, current + sums, where, 1)


def channel_plan(queries, keys, values, filters, cotangent):
    rows, width = queries.shape
    nfil = filters.shape[0]
    gated = (keys.astype(jnp.float32) * values.astype(jnp.float32)).astype(jnp.bfloat16)
    back = (cotangent.astype(jnp.float32) * queries.astype(jnp.float32)).astype(jnp.bfloat16)
    taps = lax.all_gather(filters, "ctx", axis=1, tiled=True)
    total = taps.shape[1]
    padded = jnp.concatenate([jnp.zeros_like(taps), taps], axis=1)
    lag_start = jnp.zeros((nfil, 2 * total), jnp.float32)
    chan_gated, chan_back = (
        lax.all_to_all(gated, "ctx", split_axis=1, concat_axis=0, tiled=True),
        lax.all_to_all(back, "ctx", split_axis=1, concat_axis=0, tiled=True),
    )
    blocks = total // rows
    slim = chan_gated.shape[1] // nfil
    gated_cols = chan_gated.reshape(blocks, rows, slim, nfil)
    back_cols = chan_back.reshape(blocks, rows, slim, nfil)
    gated_pad = jnp.concatenate([jnp.zeros_like(gated_cols), gated_cols], axis=0)
    back_pad = jnp.concatenate([back_cols, jnp.zeros_like(back_cols)], axis=0)

    def turn(offset, carry):
        mixed_acc, grad_acc, lag_acc = carry
        tile = toeplitz(padded, offset * rows, rows, rows)
        earlier = lax.dynamic_slice_in_dim(gated_pad, blocks - offset, blocks, 0)
        later = lax.dynamic_slice_in_dim(back_pad, offset, blocks, 0)
        mixed_acc = mixed_acc + jnp.einsum(
            "fst,ntcf->nscf", tile, earlier, preferred_element_type=jnp.float32
        )
        grad_acc = grad_acc + jnp.einsum(
            "fst,nscf->ntcf", tile, later, preferred_element_type=jnp.float32
        )
        product = jnp.einsum(
            "nscf,ntcf->fst", back_cols, earlier, preferred_element_type=jnp.float32
        )
        lag_acc = add_lags(lag_acc, diagonal_sums(product), offset * rows - rows + 1)
        return (mixed_acc, grad_acc, lag_acc)

    blank = jnp.zeros((blocks, rows, slim, nfil), jnp.float32)
    mixed_acc, grad_acc, lag_part = lax.fori_loop(0, blocks, turn, (blank, blank, lag_start))
    mixed_chan = mixed_acc.reshape(total, slim * nfil)
    grad_chan = grad_acc.reshape(total, slim * nfil)
    mixed, gated_grad = (
        lax.all_to_all(mixed_chan, "ctx", split_axis=0, concat_axis=1, tiled=True),
        lax.all_to_all(grad_chan, "ctx", split_axis=0, concat_axis=1, tiled=True),
    )
    lag_share = lax.psum_scatter(
        lag_part[:, total:].astype(jnp.bfloat16), "ctx", scatter_dimension=1, tiled=True
    ).astype(jnp.float32)
    lag_total = lax.psum(lag_share, "chan")
    scale = (total * (D // NFILT)) ** (-0.5)
    filter_grad = lag_total * scale
    output = (queries.astype(jnp.float32) * mixed).astype(jnp.bfloat16)
    query_grad = (cotangent.astype(jnp.float32) * mixed).astype(jnp.bfloat16)
    key_grad = (gated_grad * values.astype(jnp.float32)).astype(jnp.bfloat16)
    value_grad = (gated_grad * keys.astype(jnp.float32)).astype(jnp.bfloat16)
    return (output, query_grad, key_grad, value_grad, filter_grad)


def solution(mesh):
    count, chans = mesh.shape["ctx"], mesh.shape["chan"]

    def shards(queries, keys, values, filters, cotangent):
        width = queries.shape[1]
        quarter = width // max(count // 2, 1)
        if count == 8 and chans == 4 and quarter % (2 * LANES) == 0 and queries.shape[0] == LANES:
            return halves_plan(count, chans, queries, keys, values, filters, cotangent)
        return channel_plan(queries, keys, values, filters, cotangent)

    wide = P("ctx", "chan")
    return jax.shard_map(
        shards,
        mesh=mesh,
        in_specs=(wide, wide, wide, P(None, "ctx"), wide),
        out_specs=(wide, wide, wide, wide, P(None, "ctx")),
        check_vma=False,
    )
```

```python
import functools

import jax
import jax.numpy as jnp
from jax import lax
from jax.experimental import pallas as pl
from jax.experimental.pallas import tpu as pltpu
from jax.sharding import PartitionSpec as P

D = 8192
NFILT = 4
LANES = 128
GRANT = 24 * 2**20


def exchange(size, reverse, dtype):
    row = lax.broadcasted_iota(jnp.int32, (size, size), 0)
    col = lax.broadcasted_iota(jnp.int32, (size, size), 1)
    target = jnp.where(reverse, size - 1 - row, row)
    return jnp.where(col == target, 1.0, 0.0).astype(jnp.float32).astype(dtype)


def exact_rows(matrix, values):
    return jnp.dot(matrix, values, preferred_element_type=jnp.float32).astype(jnp.bfloat16)


def gate_kernel(half, slim, me_ref, q_ref, k_ref, v_ref, g_ref, *refs):
    outs, (held, sems) = refs[:-2], refs[-2:]
    rows = q_ref.shape[0]
    me = me_ref[0]
    upper = me >= half
    copies = []
    for chunk in range(half // 2):
        base = (((me & (half - 1)) // 2) ^ chunk) * 2 * slim
        lanes = pl.ds(pl.multiple_of(base, LANES), 2 * slim)
        copies.append([])
        for index, ref in enumerate((q_ref, k_ref, v_ref, g_ref)):
            copy = pltpu.make_async_copy(
                ref.at[:, lanes], held.at[chunk, index], sems.at[chunk, index]
            )
            copy.start()
            copies[chunk].append(copy)
    turn = exchange(rows, upper, jnp.bfloat16)
    turn_other = exchange(rows, jnp.logical_not(upper), jnp.bfloat16)
    for step in range(half):
        if step % 2 == 0:
            for copy in copies[step // 2]:
                copy.wait()
        lanes = pl.ds(pl.multiple_of(((me ^ step) & 1) * slim, LANES), slim)
        q, k, v, g = [held[step // 2, index, :, lanes].astype(jnp.float32) for index in range(4)]
        gated = (k * v).astype(jnp.bfloat16)
        back = (g * q).astype(jnp.bfloat16)
        second = jnp.where(upper, back, gated)
        outs[step][...] = exact_rows(turn_other, second)
        bundle = outs[half + step]
        bundle[0:rows, :] = exact_rows(turn, jnp.where(upper, gated, back))
        bundle[rows : 2 * rows, :] = exact_rows(turn, second)


def label_kernel(half, me_ref, mine_ref, other_ref, *refs):
    outs, (held, sems) = refs[half : 2 * half], refs[2 * half :]
    rows = outs[0].shape[0] - 16
    mine, other = mine_ref[...].astype(jnp.float32), other_ref[...].astype(jnp.float32)
    gap = jnp.zeros((8 - mine.shape[0], LANES), jnp.float32)
    held[...] = jnp.zeros(held.shape, jnp.bfloat16)
    held[:, 0:LANES] = jnp.concatenate([mine, gap, other, gap], axis=0).astype(jnp.bfloat16)
    copies = [
        pltpu.make_async_copy(held, outs[step].at[rows : rows + 16], sems.at[step])
        for step in range(half)
    ]
    for copy in copies:
        copy.start()
    for copy in copies:
        copy.wait()


def fill_bands(half, me, arrived, near_ref, far_ref, line):
    nfil, size, total = near_ref.shape
    for step in range(half):
        both = arrived[step][arrived[step].shape[0] - 16 :, 0:LANES].astype(jnp.float32)
        for index, source in enumerate((me ^ step, me ^ step ^ half)):
            place = pl.multiple_of(source * LANES, LANES)
            line[:, pl.ds(place, LANES)] = both[8 * index : 8 * index + 8, :]
    row = lax.broadcasted_iota(jnp.int32, (size, total), 0)
    col = lax.broadcasted_iota(jnp.int32, (size, total), 1)
    reach = far_ref.shape[2] // size
    for index in range(nfil):
        spread = jnp.broadcast_to(line[index : index + 1, :], (size, total))
        rolled = pltpu.roll(spread, 0, 1, stride=1, stride_axis=0)
        band = jnp.where(col >= row, rolled, 0.0)
        near_ref[index] = band.astype(jnp.bfloat16)
        for block in range(reach):
            piece = band[:, (reach - 1 - block) * size : (reach - block) * size]
            far_ref[index, :, block * size : (block + 1) * size] = piece.T.astype(jnp.bfloat16)


def slot_of(half, me, step):
    return ((me ^ step) & (half - 1)) ^ jnp.where(me >= half, half - 1, 0)


def rows_at(slot, rows):
    return pl.ds(pl.multiple_of(slot * rows, rows), rows)


def products(left, right):
    contract = (((1,), (1,)), ((), ()))
    return lax.dot_general(left, right, contract, preferred_element_type=jnp.float32)


def add_columns(columns, values, start):
    first = start // LANES
    for index in range(values.shape[1] // LANES):
        piece = values[:, index * LANES : (index + 1) * LANES]
        have = columns[first + index]
        columns[first + index] = piece if have is None else have + piece


def joined_columns(columns, rows):
    blank = jnp.zeros((rows, LANES), jnp.float32)
    return jnp.concatenate([blank if c is None else c for c in columns], axis=1)


def diagonal_rows(acc):
    rolled = pltpu.roll(acc, 0, 1, stride=1, stride_axis=0)
    return jnp.broadcast_to(jnp.sum(rolled, axis=0, keepdims=True), (8, acc.shape[1]))


def pair_base(half, me, pair, rows):
    slot = slot_of(half, me, 2 * pair)
    return pl.multiple_of((slot // 2) * 2 * rows, 2 * rows)


def stack_pair(half, me, pair, arrived, target, rows):
    for index in range(2):
        place = (slot_of(half, me, 2 * pair + index) % 2) * rows
        target[pl.ds(pl.multiple_of(place, rows), rows), :] = arrived[index][...]


def outer_lags(half, me, base, pair_ref, flip_ref, lag_ref):
    own, width = flip_ref.shape
    rows = own // half
    reach = pair_ref.shape[0]
    share = width // 2
    window = own + reach
    lanes = pl.ds(pl.multiple_of(jnp.where(me >= half, share, 0), LANES), share)
    for index in range(NFILT):
        right = pair_ref[:, lanes] * lane_mask(share, NFILT, index)
        columns = [None] * (window // LANES)
        every = products(flip_ref[:, lanes], right)
        for start in range(0, own, rows):
            add_columns(columns, every[start : start + rows, :], own - rows - start)
        sums = pltpu.roll(diagonal_rows(joined_columns(columns, rows)), 1, 1)
        lag_ref[index : index + 1, pl.ds(base, window)] += sums[0:1, :]


def outer_rows(half, top, base, near_ref, pair_ref):
    nfil, size, total = near_ref.shape
    reach, width = pair_ref.shape
    acc = jnp.zeros((size, width), jnp.float32)
    for index in range(nfil):
        start = pl.multiple_of(total // 2 - top + base, reach)
        acc += jnp.dot(
            near_ref[index, :, pl.ds(start, reach)],
            pair_ref[...] * lane_mask(width, nfil, index),
            preferred_element_type=jnp.float32,
        )
    return acc


def lane_mask(width, nfil, index):
    lane = lax.broadcasted_iota(jnp.int32, (1, width), 1)
    return jnp.where(lane % nfil == index, 1.0, 0.0).astype(jnp.bfloat16)


def inner_kernel(half, me_ref, *refs):
    arrived, across = refs[:half], (refs[half + 1], refs[half])
    outs = refs[half + 2 : 2 * half + 2]
    near_ref, part_ref, flip_ref, lag_ref = refs[2 * half + 2 : 2 * half + 6]
    far_ref, line, first_ref, second_ref, pair_ref, result_ref = refs[2 * half + 6 :]
    nfil, size, total = near_ref.shape
    own, width = second_ref.shape
    rows = own // half
    me = me_ref[0]
    turn = exchange(rows, True, jnp.bfloat16)
    fill_bands(half, me, arrived, near_ref, far_ref, line)
    for step in range(half):
        where = rows_at(slot_of(half, me, step), rows)
        first_ref[where, :] = arrived[step][0:rows, :]
        second_ref[where, :] = arrived[step][rows : 2 * rows, :]
        flip_ref[where, :] = exact_rows(turn, arrived[step][rows : 2 * rows, :])
    stack_pair(half, me, 0, across, pair_ref, rows)
    base = pair_base(half, me, 0, rows)
    masks = [lane_mask(width, nfil, index) for index in range(nfil)]
    for top in range(0, own, size):
        acc = jnp.zeros((size, width), jnp.float32)
        for index in range(nfil):
            acc += jnp.dot(
                far_ref[index, :, own - size - top : own],
                second_ref[0 : top + size, :] * masks[index],
                preferred_element_type=jnp.float32,
            )
        result_ref[top : top + size, :] = acc.astype(jnp.bfloat16)
    for step in range(half):
        outs[step][...] = result_ref[rows_at(slot_of(half, me, step), rows), :]
    for top in range(0, own, size):
        acc = outer_rows(half, top, base, near_ref, pair_ref)
        for index in range(nfil):
            acc += jnp.dot(
                near_ref[index, :, 0 : own - top],
                first_ref[top:own, :] * masks[index],
                preferred_element_type=jnp.float32,
            )
        part_ref[top : top + size, :] = acc
    lag_ref[...] = jnp.zeros((8, total), jnp.float32)
    for index in range(nfil):
        columns = [None] * ((own + rows) // LANES)
        every = products(flip_ref[...], first_ref[...] * masks[index])
        for start in range(0, own, rows):
            add_columns(columns, every[start : start + rows, start:own], 0)
        sums = pltpu.roll(diagonal_rows(joined_columns(columns, rows)), own + 1, 1)
        lag_ref[index : index + 1, 0:own] = sums[0:1, 0:own]
    outer_lags(half, me, base, pair_ref, flip_ref, lag_ref)


def lag_kernel(half, me_ref, *refs):
    across = refs[:2]
    flip_ref, lag_ref, out_ref, pair_ref = refs[2:]
    rows = flip_ref.shape[0] // half
    me = me_ref[0]
    stack_pair(half, me, 1, across, pair_ref, rows)
    out_ref[...] = lag_ref[...]
    outer_lags(half, me, pair_base(half, me, 1, rows), pair_ref, flip_ref, out_ref)


def attach_kernel(half, me_ref, lag_ref, *refs):
    outs, (held, sems) = refs[half : 2 * half], refs[2 * half :]
    rows = outs[0].shape[0] - 16
    nfil = NFILT
    me = me_ref[0]
    copies = []
    for step in range(half):
        pieces = []
        for target in (me ^ step, me ^ step ^ half):
            place = pl.multiple_of(target * LANES, LANES)
            pieces.append(lag_ref[0:nfil, pl.ds(place, LANES)])
        both = jnp.concatenate(pieces, axis=0)
        high = both.astype(jnp.bfloat16).astype(jnp.float32)
        rest = (both - high).astype(jnp.bfloat16).astype(jnp.float32)
        held[step] = jnp.zeros(held.shape[1:], jnp.bfloat16)
        held[step, :, 0:LANES] = jnp.concatenate([high, rest], axis=0).astype(jnp.bfloat16)
        copy = pltpu.make_async_copy(held.at[step], outs[step].at[rows : rows + 16], sems.at[step])
        copy.start()
        copies.append(copy)
    for copy in copies:
        copy.wait()


def outer_kernel(half, me_ref, *refs):
    across = refs[:2]
    near_ref, part_ref = refs[2:4]
    outs = refs[4 : half + 4]
    pair_ref, result_ref = refs[half + 4 :]
    nfil, size, total = near_ref.shape
    own, width = part_ref.shape
    rows = own // half
    me = me_ref[0]
    stack_pair(half, me, 1, across, pair_ref, rows)
    base = pair_base(half, me, 1, rows)
    for top in range(0, own, size):
        acc = part_ref[top : top + size, :] + outer_rows(half, top, base, near_ref, pair_ref)
        result_ref[top : top + size, :] = acc.astype(jnp.bfloat16)
    for step in range(half):
        outs[step][0:rows, :] = result_ref[rows_at(slot_of(half, me, step), rows), :]


def final_kernel(half, slim, me_ref, q_ref, k_ref, v_ref, g_ref, *refs):
    firsts = [refs[0], *refs[half - 1 : 0 : -1]]
    seconds = [refs[half], *refs[2 * half - 1 : half : -1]]
    outs = refs[2 * half : 2 * half + 4]
    held, sems = refs[2 * half + 4 :]
    rows = q_ref.shape[0]
    me = me_ref[0]
    upper = me >= half
    turn = exchange(rows, upper, jnp.bfloat16)
    copies = []
    for step in range(half):
        part = (me ^ step) & (half - 1)
        lanes = pl.ds(pl.multiple_of(part * slim, LANES), slim)
        first = jnp.dot(turn, firsts[step][0:rows, :], preferred_element_type=jnp.float32)
        second = jnp.dot(turn, seconds[step][...], preferred_element_type=jnp.float32)
        mixed = jnp.where(upper, first, second)
        grad = jnp.where(upper, second, first)
        for index, (ref, value) in enumerate(
            ((q_ref, mixed), (g_ref, mixed), (v_ref, grad), (k_ref, grad))
        ):
            held[step, index] = (ref[:, lanes].astype(jnp.float32) * value).astype(jnp.bfloat16)
            copy = pltpu.make_async_copy(
                held.at[step, index], outs[index].at[:, lanes], sems.at[step, index]
            )
            copy.start()
            copies.append(copy)
    for copy in copies:
        copy.wait()


def swap(value, step, count):
    return lax.ppermute(value, "ctx", [(i, i ^ step) for i in range(count)])


def after(value, *earlier):
    return lax.optimization_barrier((value, *earlier))


def call(kernel, outs, scratch, flops, nbytes, *args, far=0, far_out=False, alias=0):
    near_spec, far_spec = pl.BlockSpec(memory_space=pltpu.VMEM), pl.BlockSpec(memory_space=pl.ANY)
    near = len(args) - 1 - far - alias
    return pl.pallas_call(
        kernel,
        out_shape=outs,
        in_specs=[pl.BlockSpec(memory_space=pltpu.SMEM)]
        + [far_spec] * far
        + [near_spec] * near
        + [far_spec] * alias,
        out_specs=[far_spec if far_out else near_spec] * len(outs),
        scratch_shapes=scratch,
        input_output_aliases={len(args) - alias + k: k for k in range(alias)},
        compiler_params=pltpu.CompilerParams(vmem_limit_bytes=GRANT),
        cost_estimate=pl.CostEstimate(flops=flops, bytes_accessed=nbytes, transcendentals=0),
    )(*args)


def halves_plan(count, chans, queries, keys, values, filters, cotangent):
    rows, width = queries.shape
    nfil = filters.shape[0]
    half = count // 2
    slim = width // half
    total = count * rows
    own = half * rows
    size = min(256, own)
    low = jnp.bfloat16
    shape = jax.ShapeDtypeStruct
    me = lax.axis_index("ctx")
    where = me.astype(jnp.int32).reshape(1)

    other_taps = swap(filters, half, count)
    branches = [
        pltpu.with_memory_space_constraint(x, pltpu.HBM)
        for x in (queries, keys, values, cotangent)
    ]
    made = call(
        functools.partial(gate_kernel, half, slim),
        [shape((rows, slim), low)] * half + [shape((2 * rows + 16, slim), low)] * half,
        [pltpu.VMEM((half // 2, 4, rows, 2 * slim), low), pltpu.SemaphoreType.DMA((half // 2, 4))],
        2 * rows * rows * width,
        14 * rows * width,
        where, *branches, far=4,
    )
    sent = made[:half]
    inner = call(
        functools.partial(label_kernel, half),
        [shape((2 * rows + 16, slim), low)] * half,
        [pltpu.VMEM((16, slim), low), pltpu.SemaphoreType.DMA((half,))],
        0,
        64 * slim * half,
        where, filters, other_taps, *made[half:], alias=half, far_out=True,
    )
    inner = [inner[0]] + [swap(inner[k], k, count) for k in range(1, half)]
    outer = list(sent)
    outer[1] = swap(outer[1], half + 1, count)
    outer[0] = swap(outer[0], half, count)
    outer[2], inner[1] = after(outer[2], inner[1])
    outer[2] = swap(outer[2], half + 2, count)
    outer[3], inner[2] = after(outer[3], inner[2])
    outer[3] = swap(outer[3], half + 3, count)

    *second, near, part, flipped, lags = call(
        functools.partial(inner_kernel, half),
        [shape((rows, slim), low)] * half
        + [
            shape((nfil, size, total), low),
            shape((own, slim), jnp.float32),
            shape((own, slim), low),
            shape((8, total), jnp.float32),
        ],
        [
            pltpu.VMEM((nfil, size, own), low),
            pltpu.VMEM((8, total), jnp.float32),
            pltpu.VMEM((own, slim), low),
            pltpu.VMEM((own, slim), low),
            pltpu.VMEM((2 * rows, slim), low),
            pltpu.VMEM((own, slim), low),
        ],
        8 * nfil * own * slim * own,
        8 * own * slim,
        where, *inner, outer[1], outer[0],
    )
    second = [second[0]] + [swap(second[k], k, count) for k in range(half - 1, 0, -1)][::-1]
    across = lambda value, move, turn: lax.ppermute(
        value,
        ("chan", "ctx"),
        [(c * count + i, (c ^ move) * count + (i ^ turn)) for c in range(chans) for i in range(count)],
    )
    (lags,) = call(
        functools.partial(lag_kernel, half),
        [shape((8, total), jnp.float32)],
        [pltpu.VMEM((2 * rows, slim), low)],
        nfil * own * slim * own // 2,
        own * slim,
        where, *outer[2:], flipped, lags,
    )
    outer[2], lags = after(outer[2], lags)
    first = call(
        functools.partial(outer_kernel, half),
        [shape((rows + 16, slim), low)] * half,
        [pltpu.VMEM((2 * rows, slim), low), pltpu.VMEM((own, slim), low)],
        nfil * own * slim * own,
        4 * own * slim,
        where, *outer[2:], near, part,
    )
    lags = lags + across(lags, 1, 0)
    first = call(
        functools.partial(attach_kernel, half),
        [shape((rows + 16, slim), low)] * half,
        [pltpu.VMEM((half, 16, slim), low), pltpu.SemaphoreType.DMA((half,))],
        0,
        32 * slim * half,
        where, lags, *first, alias=half, far_out=True,
    )
    first = [first[0]] + [swap(first[k], k, count) for k in range(half - 1, 0, -1)][::-1]
    sums = sum(value[rows:, 0:LANES].astype(jnp.float32) for value in first)
    sums = sums[: 2 * nfil] + sums[2 * nfil :]
    mine, other = sums[:nfil], sums[nfil:]
    scale = (total * (D // NFILT)) ** (-0.5)
    arrived = [across(other, 0, half), across(mine, 2, 0), across(other, 2, half)]
    filter_grad = (mine + sum(arrived)) * scale

    outs = call(
        functools.partial(final_kernel, half, slim),
        [shape((rows, width), low)] * 4,
        [pltpu.VMEM((half, 4, rows, slim), low), pltpu.SemaphoreType.DMA((half, 4))],
        4 * rows * rows * width,
        20 * rows * width,
        where, queries, keys, values, cotangent, first[0], *first[:0:-1], second[0], *second[:0:-1], far_out=True,
    )
    return (*outs, filter_grad)


def toeplitz(padded, base, height, breadth):
    middle = padded.shape[1] // 2
    span = height + breadth - 1
    window = lax.dynamic_slice_in_dim(padded, middle + base - breadth + 1, span, 1)
    flipped = window[:, ::-1]
    tiled = jnp.tile(flipped, (1, height + 1))
    flat = tiled[:, height - 1 : height - 1 + height * (span - 1)]
    return flat.reshape(padded.shape[0], height, span - 1)[:, :, :breadth]


def diagonal_sums(product):
    nfil, height, breadth = product.shape
    stride = height + breadth
    flipped = product[:, :, ::-1]
    padded = jnp.pad(flipped, ((0, 0), (0, 0), (0, height)))
    flat = padded.reshape(nfil, height * stride)[:, : height * (stride - 1)]
    return jnp.sum(flat.reshape(nfil, height, stride - 1), axis=1)


def add_lags(lag_acc, sums, first_lag):
    middle = lag_acc.shape[1] // 2
    where = middle + first_lag
    current = lax.dynamic_slice_in_dim(lag_acc, where, sums.shape[1], 1)
    return lax.dynamic_update_slice_in_dim(lag_acc, current + sums, where, 1)


def channel_plan(queries, keys, values, filters, cotangent):
    rows, width = queries.shape
    nfil = filters.shape[0]
    gated = (keys.astype(jnp.float32) * values.astype(jnp.float32)).astype(jnp.bfloat16)
    back = (cotangent.astype(jnp.float32) * queries.astype(jnp.float32)).astype(jnp.bfloat16)
    taps = lax.all_gather(filters, "ctx", axis=1, tiled=True)
    total = taps.shape[1]
    padded = jnp.concatenate([jnp.zeros_like(taps), taps], axis=1)
    lag_start = jnp.zeros((nfil, 2 * total), jnp.float32)
    chan_gated, chan_back = (
        lax.all_to_all(gated, "ctx", split_axis=1, concat_axis=0, tiled=True),
        lax.all_to_all(back, "ctx", split_axis=1, concat_axis=0, tiled=True),
    )
    blocks = total // rows
    slim = chan_gated.shape[1] // nfil
    gated_cols = chan_gated.reshape(blocks, rows, slim, nfil)
    back_cols = chan_back.reshape(blocks, rows, slim, nfil)
    gated_pad = jnp.concatenate([jnp.zeros_like(gated_cols), gated_cols], axis=0)
    back_pad = jnp.concatenate([back_cols, jnp.zeros_like(back_cols)], axis=0)

    def turn(offset, carry):
        mixed_acc, grad_acc, lag_acc = carry
        tile = toeplitz(padded, offset * rows, rows, rows)
        earlier = lax.dynamic_slice_in_dim(gated_pad, blocks - offset, blocks, 0)
        later = lax.dynamic_slice_in_dim(back_pad, offset, blocks, 0)
        mixed_acc = mixed_acc + jnp.einsum(
            "fst,ntcf->nscf", tile, earlier, preferred_element_type=jnp.float32
        )
        grad_acc = grad_acc + jnp.einsum(
            "fst,nscf->ntcf", tile, later, preferred_element_type=jnp.float32
        )
        product = jnp.einsum(
            "nscf,ntcf->fst", back_cols, earlier, preferred_element_type=jnp.float32
        )
        lag_acc = add_lags(lag_acc, diagonal_sums(product), offset * rows - rows + 1)
        return (mixed_acc, grad_acc, lag_acc)

    blank = jnp.zeros((blocks, rows, slim, nfil), jnp.float32)
    mixed_acc, grad_acc, lag_part = lax.fori_loop(0, blocks, turn, (blank, blank, lag_start))
    mixed_chan = mixed_acc.reshape(total, slim * nfil)
    grad_chan = grad_acc.reshape(total, slim * nfil)
    mixed, gated_grad = (
        lax.all_to_all(mixed_chan, "ctx", split_axis=0, concat_axis=1, tiled=True),
        lax.all_to_all(grad_chan, "ctx", split_axis=0, concat_axis=1, tiled=True),
    )
    lag_share = lax.psum_scatter(
        lag_part[:, total:].astype(jnp.bfloat16), "ctx", scatter_dimension=1, tiled=True
    ).astype(jnp.float32)
    lag_total = lax.psum(lag_share, "chan")
    scale = (total * (D // NFILT)) ** (-0.5)
    filter_grad = lag_total * scale
    output = (queries.astype(jnp.float32) * mixed).astype(jnp.bfloat16)
    query_grad = (cotangent.astype(jnp.float32) * mixed).astype(jnp.bfloat16)
    key_grad = (gated_grad * values.astype(jnp.float32)).astype(jnp.bfloat16)
    value_grad = (gated_grad * keys.astype(jnp.float32)).astype(jnp.bfloat16)
    return (output, query_grad, key_grad, value_grad, filter_grad)


def solution(mesh):
    count, chans = mesh.shape["ctx"], mesh.shape["chan"]

    def shards(queries, keys, values, filters, cotangent):
        width = queries.shape[1]
        quarter = width // max(count // 2, 1)
        if count == 8 and chans == 4 and quarter % (2 * LANES) == 0 and queries.shape[0] == LANES:
            return halves_plan(count, chans, queries, keys, values, filters, cotangent)
        return channel_plan(queries, keys, values, filters, cotangent)

    wide = P("ctx", "chan")
    return jax.shard_map(
        shards,
        mesh=mesh,
        in_specs=(wide, wide, wide, P(None, "ctx"), wide),
        out_specs=(wide, wide, wide, wide, P(None, "ctx")),
        check_vma=False,
    )
```
